256 devices in a mesh: dp: 2 (over core), inp: 4 (over y), out: 32 (over z, x).
Axes of the slice: x: 4, y: 4, z: 8, core: 2. Of those that a mesh axis runs over, the one named last changes fastest.
Arguments:
- inputs: bfloat16 [2048, 8192], P('dp', 'inp'), may hold values from -6 to 6
- gate_pre: bfloat16 [2048, 28672], P('dp', 'out'), may hold values from -8 to 8
- up_pre: bfloat16 [2048, 28672], P('dp', 'out'), may hold values from -6 to 6
- upstream: bfloat16 [2048, 28672], P('dp', 'out'), may hold values from -6 to 6
- gate_weight: bfloat16 [8192, 28672], P('inp', 'out'), may hold values from -0.0625 to 0.0625
- up_weight: bfloat16 [8192, 28672], P('inp', 'out'), may hold values from -0.0625 to 0.0625
- a_down: bfloat16 [16, 8192], P(None, 'inp'), may hold values from -0.0625 to 0.0625
- b_gate: bfloat16 [16, 28672], P(None, 'out'), may hold values from -1.5 to 1.5
- b_up: bfloat16 [16, 28672], P(None, 'out'), may hold values from -1.5 to 1.5
- probe_a: bfloat16 [16, 8192], P(None, 'inp'), may hold values from -0.0625 to 0.0625
- probe_bg: bfloat16 [16, 28672], P(None, 'out'), may hold values from -1.5 to 1.5
- probe_bu: bfloat16 [16, 28672], P(None, 'out'), may hold values from -1.5 to 1.5
Outputs:
- input_tangent: float32 [2048, 8192], P(('dp', 'out'), 'inp')
- next_a: float32 [16, 8192], P(None, 'inp')
- next_bg: float32 [16, 28672], P(None, 'out')
- next_bu: float32 [16, 28672], P(None, 'out')
The draws below stay inside these ranges and needn't reach their ends.
All inputs are finite; a program needn't handle non-finite values.
Results may differ from the reference program's by a relative error of at most 0.0025.
Values sent between devices are 32-bit elements; how exact they have to be, the bound alone decides.
No kernel may reach another device: no remote copies, remote signals or barrier semaphores. Data moves between devices by JAX's collectives and lax.ppermute only.
A program may use at most 128 MiB of HBM per device.

```python
import math
import jax
import jax.numpy as jnp
from jax import lax

D = 8192
FF = 28672
R = 16
TOKENS = 2048


def shard_levels(own_key, extent, pieces, smallest, high):
    def one(position, shards_of):
        heights = jax.random.uniform(jax.random.fold_in(jax.random.fold_in(own_key, 6), position), (shards_of,), jnp.float32, smallest / len(pieces), high / len(pieces))
        return jnp.repeat(jnp.exp(heights), extent[position] // shards_of).reshape((-1,) + (1,) * (len(extent) - position - 1))

    level = one(*pieces[0])
    for cut in pieces[1:]:
        level = level * one(*cut)
    return level


def bell_draw(stream_key, dims, spread, bound, cuts=(), held_as=jnp.bfloat16):
    factor_of = shard_levels(stream_key, dims, cuts, -0.22, 0.18) if cuts else 1.0
    array = jax.random.normal(stream_key, dims, jnp.float32) * spread * factor_of
    return jnp.minimum(jnp.maximum(array, -bound), bound).astype(held_as)


def setup_inputs(seed: int = 0) -> dict:
    arg_keys = jax.random.split(jax.random.key(seed), 13)
    inputs = bell_draw(arg_keys[0], (TOKENS, D), 1.0, 6.0, ((0, 2), (1, 4)))
    gate_pre = bell_draw(arg_keys[1], (TOKENS, FF), 2.0, 8.0, ((0, 2), (1, 32)))
    up_pre = bell_draw(arg_keys[2], (TOKENS, FF), 1.0, 6.0, ((0, 2), (1, 32)))
    upstream = bell_draw(arg_keys[3], (TOKENS, FF), 1.0, 6.0, ((0, 2), (1, 32)))
    gate_weight = bell_draw(arg_keys[4], (D, FF), D ** -0.5, 0.0625, ((0, 4), (1, 32)))
    up_weight = bell_draw(arg_keys[5], (D, FF), D ** -0.5, 0.0625, ((0, 4), (1, 32)))
    a_down = bell_draw(arg_keys[6], (R, D), D ** -0.5, 0.0625, ((1, 4),))
    b_gate = bell_draw(arg_keys[7], (R, FF), 0.25, 1.5, ((1, 32),))
    b_up = bell_draw(arg_keys[8], (R, FF), 0.25, 1.5, ((1, 32),))
    probe_a = bell_draw(arg_keys[9], (R, D), D ** -0.5, 0.0625, ((1, 4),))
    probe_bg = bell_draw(arg_keys[10], (R, FF), 0.25, 1.5, ((1, 32),))
    probe_bu = bell_draw(arg_keys[11], (R, FF), 0.25, 1.5, ((1, 32),))
    return dict(inputs=inputs, gate_pre=gate_pre, up_pre=up_pre, upstream=upstream, gate_weight=gate_weight, up_weight=up_weight, a_down=a_down, b_gate=b_gate, b_up=b_up, probe_a=probe_a, probe_bg=probe_bg, probe_bu=probe_bu)


def reference(inputs, gate_pre, up_pre, upstream, gate_weight, up_weight, a_down, b_gate, b_up, probe_a, probe_bg, probe_bu):
    highest = lax.Precision.HIGHEST
    f32 = jnp.float32
    gval = gate_pre.astype(f32)
    uval = up_pre.astype(f32)
    grad_out = upstream.astype(f32)
    sig = jax.nn.sigmoid(gval)
    silu_val = gval * sig
    first = sig * (1.0 + gval * (1.0 - sig))
    second = sig * (1.0 - sig) * (2.0 + gval * (1.0 - 2.0 * sig))
    xa_rank = jnp.dot(inputs, a_down.T, preferred_element_type=f32)
    xv_rank = jnp.dot(inputs, probe_a.T, preferred_element_type=f32)
    tang_g = jnp.dot(xv_rank, b_gate.astype(f32), precision=highest) + jnp.dot(xa_rank, probe_bg.astype(f32), precision=highest)
    tang_u = jnp.dot(xv_rank, b_up.astype(f32), precision=highest) + jnp.dot(xa_rank, probe_bu.astype(f32), precision=highest)
    grad_g = grad_out * uval * first
    grad_u = grad_out * silu_val
    tgg = (grad_out * (tang_u * first + uval * second * tang_g)).astype(jnp.bfloat16)
    tgu = (grad_out * first * tang_g).astype(jnp.bfloat16)
    p_rank = jnp.dot(tgg, b_gate.T, preferred_element_type=f32) + jnp.dot(tgu, b_up.T, preferred_element_type=f32) + jnp.dot(grad_g, probe_bg.astype(f32).T, precision=highest) + jnp.dot(grad_u, probe_bu.astype(f32).T, precision=highest)
    q_rank = jnp.dot(grad_g, b_gate.astype(f32).T, precision=highest) + jnp.dot(grad_u, b_up.astype(f32).T, precision=highest)
    wide = jnp.dot(tgg, gate_weight.T, preferred_element_type=f32) + jnp.dot(tgu, up_weight.T, preferred_element_type=f32)
    input_tangent = wide + jnp.dot(p_rank, a_down.astype(f32), precision=highest) + jnp.dot(q_rank, probe_a.astype(f32), precision=highest)
    hvp_bg = jnp.dot(xv_rank.T, grad_g, precision=highest) + jnp.dot(xa_rank.T, tgg.astype(f32), precision=highest)
    hvp_bu = jnp.dot(xv_rank.T, grad_u, precision=highest) + jnp.dot(xa_rank.T, tgu.astype(f32), precision=highest)
    hvp_a = jnp.dot(p_rank.T, inputs.astype(f32), precision=highest)
    scale_b = math.sqrt(TOKENS)
    scale_a = math.sqrt(TOKENS * FF)
    next_a = 2.0 * probe_a.astype(f32) - hvp_a / scale_a
    next_bg = 2.0 * probe_bg.astype(f32) - hvp_bg / scale_b
    next_bu = 2.0 * probe_bu.astype(f32) - hvp_bu / scale_b
    return (input_tangent, next_a, next_bg, next_bu)
```

```python
import functools
import math

import jax
import jax.numpy as jnp
from jax import lax
from jax.experimental import pallas as pl
from jax.experimental.pallas import tpu as pltpu
from jax.sharding import PartitionSpec as P

FF = 28672
NX, NZ = 4, 8
F32, BF16 = jnp.float32, jnp.bfloat16
VMEM_LIMIT = 26 * 1024 * 1024
LANES = 128


def dot_nt(left, right):
    return lax.dot_general(left, right, (((1,), (1,)), ((), ())), preferred_element_type=F32)


def dot_nn(left, right):
    return lax.dot_general(left, right, (((1,), (0,)), ((), ())), preferred_element_type=F32)


def dot_tn(left, right):
    return lax.dot_general(left, right, (((0,), (0,)), ((), ())), preferred_element_type=F32)


def split2(value):
    high = value.astype(BF16)
    return high, (value - high.astype(F32)).astype(BF16)


def split3(value):
    high = value.astype(BF16)
    rest = value - high.astype(F32)
    mid = rest.astype(BF16)
    return high, mid, (rest - mid.astype(F32)).astype(BF16)


def params(**kw):
    return pltpu.CompilerParams(vmem_limit_bytes=VMEM_LIMIT, **kw)


def early_kernel(g_ref, u_ref, dy_ref, rg_ref, ru_ref, c1_ref, c2_ref, gu_ref, pq_ref):
    g = g_ref[...].astype(F32)
    u = u_ref[...].astype(F32)
    dy = dy_ref[...].astype(F32)
    sig = 1.0 / (1.0 + jnp.exp(-g))
    rest = 1.0 - sig
    s = g * sig
    c1 = dy * (sig + s * rest)
    c2 = dy * u * (rest * (2.0 * sig + s - 2.0 * s * sig))
    gg = c1 * u
    gu = dy * s
    c1_ref[...] = c1
    c2_ref[...] = c2
    gu_ref[...] = gu
    gg_hi, gg_lo = split2(gg)
    gu_hi, gu_lo = split2(gu)
    rg, ru = rg_ref[...], ru_ref[...]
    pq_ref[...] = (dot_nt(gg_hi, rg) + dot_nt(gg_lo, rg)) + (dot_nt(gu_hi, ru) + dot_nt(gu_lo, ru))


def early(gate_pre, up_pre, upstream, rg, ru):
    tokens, width = gate_pre.shape
    steps = 4
    block = tokens // steps
    row = pl.BlockSpec((block, width), lambda i: (i, 0))
    whole = pl.BlockSpec(rg.shape, lambda i: (0, 0))
    wide = jax.ShapeDtypeStruct((tokens, width), F32)
    return pl.pallas_call(
        early_kernel,
        grid=(steps,),
        in_specs=[row, row, row, whole, whole],
        out_specs=[row, row, row, pl.BlockSpec((block, LANES), lambda i: (i, 0))],
        out_shape=[wide, wide, wide, jax.ShapeDtypeStruct((tokens, LANES), F32)],
        compiler_params=params(),
        cost_estimate=pl.CostEstimate(flops=4_000_000_000, bytes_accessed=18_000_000, transcendentals=2_000_000),
        name="early",
    )(gate_pre, up_pre, upstream, rg, ru)


def tangent_kernel(place, c1_ref, c2_ref, tot_ref, bst_ref, pq_ref, rpg_ref, rpu_ref,
                   tgg_ref, tgu_ref, pqs_ref, pt_ref):
    width = c1_ref.shape[1]
    stack = jnp.concatenate(split3(tot_ref[...]), axis=0)
    both = dot_tn(stack, bst_ref[...])
    tang_g, tang_u = both[:, :width], both[:, width:]
    c1 = c1_ref[...]
    tgg = (tang_u * c1 + c2_ref[...] * tang_g).astype(BF16)
    tgu = (c1 * tang_g).astype(BF16)
    pq = pq_ref[...] + (dot_nt(tgg, rpg_ref[...]) + dot_nt(tgu, rpu_ref[...]))
    pt_ref[...] = pq[:, :16].T
    high = pq.astype(BF16).astype(F32)
    full = (high + pltpu.roll(pq - high, 32, 1)).astype(BF16)
    rows = tgg.shape[0] // NX
    for xx in range(NX):
        j = lax.rem(xx - place[1] + NX, NX)
        part = slice(xx * rows, (xx + 1) * rows)
        tgg_ref[0, j] = tgg[part]
        tgu_ref[0, j] = tgu[part]
        pqs_ref[0, j] = full[part]


def tangent(place, c1, c2, tot, bst, pq, rpg, rpu):
    tokens, width = c1.shape
    block = tokens // NZ
    rows = block // NX

    def nat(k, s):
        return lax.rem(k + s[0], NZ)

    row = pl.BlockSpec((block, width), lambda k, s: (nat(k, s), 0))
    rel = lambda n: pl.BlockSpec((1, NX, rows, n), lambda k, s: (k, 0, 0, 0))
    fixed = lambda a: pl.BlockSpec(a.shape, lambda k, s: (0, 0))
    return pl.pallas_call(
        tangent_kernel,
        grid_spec=pltpu.PrefetchScalarGridSpec(
            num_scalar_prefetch=1,
            grid=(NZ,),
            in_specs=[
                row, row,
                pl.BlockSpec((32, block), lambda k, s: (0, nat(k, s))),
                fixed(bst),
                pl.BlockSpec((block, LANES), lambda k, s: (nat(k, s), 0)),
                fixed(rpg), fixed(rpu),
            ],
            out_specs=[
                rel(width), rel(width), rel(LANES),
                pl.BlockSpec((16, block), lambda k, s: (0, nat(k, s))),
            ],
        ),
        out_shape=[
            jax.ShapeDtypeStruct((NZ, NX, rows, width), BF16),
            jax.ShapeDtypeStruct((NZ, NX, rows, width), BF16),
            jax.ShapeDtypeStruct((NZ, NX, rows, LANES), BF16),
            jax.ShapeDtypeStruct((16, tokens), F32),
        ],
        compiler_params=params(),
        cost_estimate=pl.CostEstimate(flops=4_000_000_000, bytes_accessed=12_000_000, transcendentals=0),
        name="tangent",
    )(place, c1, c2, tot, bst, pq, rpg, rpu)


def terms_kernel(a_list, b_list, ca, tgg_ref, tgu_ref, pqs_ref, gw_ref, uw_ref, aa_ref, *outs):
    def rows_of(ref, index):
        value = ref[index]
        return value.reshape(-1, ref.shape[-1])

    def one(indices, low, high, out_refs):
        def left(ref):
            got = [rows_of(ref, i) for i in indices]
            return got[0] if len(got) == 1 else jnp.concatenate(got, axis=0)

        lg, lu, lp = left(tgg_ref), left(tgu_ref), left(pqs_ref)
        step = 256
        n = lg.shape[0] // len(indices)
        for c in range(low, high, step):
            cols = slice(c, c + step)
            value = (dot_nt(lg, gw_ref[cols]) + dot_nt(lu, uw_ref[cols])) + dot_nt(lp, aa_ref[cols])
            for m, refs in enumerate(out_refs):
                off = c - low
                for ref in refs:
                    if off < ref.shape[1]:
                        ref[:, off:off + step] = value[m * n:(m + 1) * n]
                        break
                    off -= ref.shape[1]

    outs = list(outs)
    a_outs = [[outs.pop(0), outs.pop(0)] for _ in a_list]
    b_outs = [[outs.pop(0), outs.pop(0)] for _ in b_list]
    if a_list:
        one([(slice(None), j) for j in a_list], 0, ca, a_outs)
    if b_list:
        one([(k,) for k in b_list], ca, gw_ref.shape[0], b_outs)


def terms(a_list, b_list, ca, tgg, tgu, pqs, gw, uw, aa, name):
    nz, nx, rows, _ = tgg.shape
    cb = gw.shape[0] - ca
    shapes = []
    for _ in a_list:
        shapes += [jax.ShapeDtypeStruct((nz * rows, ca // 2), F32)] * 2
    for _ in b_list:
        shapes += [jax.ShapeDtypeStruct((nx * rows, cb // 2), F32)] * 2
    vm = pl.BlockSpec(memory_space=pltpu.VMEM)
    share = len(a_list) / 8 + len(b_list) / 16
    outs = pl.pallas_call(
        functools.partial(terms_kernel, a_list, b_list, ca),
        in_specs=[vm] * 6,
        out_specs=[vm] * len(shapes),
        out_shape=shapes,
        compiler_params=params(),
        cost_estimate=pl.CostEstimate(
            flops=int(8_000_000_000 * share), bytes_accessed=int(7_500_000 + 8_400_000 * share), transcendentals=0
        ),
        name=name,
    )(tgg, tgu, pqs, gw, uw, aa)
    outs = list(outs)
    a = {j: (outs.pop(0), outs.pop(0)) for j in a_list}
    b = {k: (outs.pop(0), outs.pop(0)) for k in b_list}
    return a, b


def factor_kernel(place, c1_ref, u_ref, gu_ref, tgg_ref, tgu_ref, tot_ref, bg_ref, bu_ref):
    k = pl.program_id(0)
    gg_hi, gg_lo = split2(c1_ref[...] * u_ref[...].astype(F32))
    gu_hi, gu_lo = split2(gu_ref[...])
    order = [lax.rem(xx - place[1] + NX, NX) for xx in range(NX)]
    tgg = jnp.concatenate([tgg_ref[0, j] for j in order], axis=0)
    tgu = jnp.concatenate([tgu_ref[0, j] for j in order], axis=0)
    t_hi, t_lo = split2(tot_ref[...])
    xv = jnp.concatenate([t_hi[:16], t_lo[:16]], axis=0)
    xa = jnp.concatenate([t_hi[16:], t_lo[16:]], axis=0)

    def both(hi, lo, tan):
        full = dot_nn(xv, hi) + dot_nn(xa, tan)
        return full[:16] + full[16:] + dot_nn(t_hi[:16], lo)

    bg = both(gg_hi, gg_lo, tgg)
    bu = both(gu_hi, gu_lo, tgu)

    @pl.when(k == 0)
    def _():
        bg_ref[...] = bg
        bu_ref[...] = bu

    @pl.when(k > 0)
    def _():
        bg_ref[...] += bg
        bu_ref[...] += bu


def factor(place, c1, up_pre, gu, tgg, tgu, tot):
    tokens, width = c1.shape
    block = tokens // NZ
    rows = block // NX

    def nat(k, s):
        return lax.rem(k + s[0], NZ)

    row = pl.BlockSpec((block, width), lambda k, s: (nat(k, s), 0))
    rel = pl.BlockSpec((1, NX, rows, width), lambda k, s: (k, 0, 0, 0))
    out = pl.BlockSpec((16, width), lambda k, s: (0, 0))
    return pl.pallas_call(
        factor_kernel,
        grid_spec=pltpu.PrefetchScalarGridSpec(
            num_scalar_prefetch=1,
            grid=(NZ,),
            in_specs=[row, row, row, rel, rel, pl.BlockSpec((32, block), lambda k, s: (0, nat(k, s)))],
            out_specs=[out, out],
        ),
        out_shape=[jax.ShapeDtypeStruct((16, width), F32)] * 2,
        compiler_params=params(),
        cost_estimate=pl.CostEstimate(flops=8_000_000_000, bytes_accessed=13_000_000, transcendentals=0),
        name="factor",
    )(place, c1, up_pre, gu, tgg, tgu, tot)


def out_perm(dz, dx):
    return [(z * NX + x, ((z + dz) % NZ) * NX + (x + dx) % NX) for z in range(NZ) for x in range(NX)]


def go_x(value, d):
    return lax.ppermute(value, "out", out_perm(0, d))


def go_z(value, d):
    return lax.ppermute(value, "out", out_perm(d, 0))


def go_y(value, d):
    return lax.ppermute(value, "inp", [(i, (i + d) % 4) for i in range(4)])


def swap_core(value):
    return lax.ppermute(value, "dp", [(0, 1), (1, 0)])


def after(value, *others):
    return lax.optimization_barrier((value,) + others)[0]


def shards(inputs, gate_pre, up_pre, upstream, gate_weight, up_weight,
           a_down, b_gate, b_up, probe_a, probe_bg, probe_bu):
    tokens = inputs.shape[0]
    ca = gate_weight.shape[0] // 2
    place_out = lax.axis_index("out")
    place = jnp.stack([place_out // NX, place_out % NX]).astype(jnp.int32)
    y = lax.axis_index("inp")
    cat0 = lambda *a: jnp.concatenate(a, axis=0)
    cat1 = lambda *a: jnp.concatenate(a, axis=1)
    lanes0 = lambda v: jnp.pad(v, ((0, LANES - v.shape[0]), (0, 0)))

    local = dot_nt(cat0(probe_a, a_down), inputs)
    across, ahead, behind = go_y(local, 2), go_y(local, 1), go_y(local, -1)
    small = cat1(cat0(b_gate, probe_bg), cat0(b_up, probe_bu))
    bst = cat0(small, small, small)
    aa = lanes0(cat0(a_down, probe_a, a_down, probe_a)).T
    c1, c2, gu, pq0 = early(
        gate_pre, up_pre, upstream, lanes0(cat0(probe_bg, b_gate)), lanes0(cat0(probe_bu, b_up))
    )
    tot = (local + across) + (ahead + behind)
    tgg, tgu, pqs, p_t = tangent(place, c1, c2, tot, bst, pq0, lanes0(b_gate), lanes0(b_up))

    def block_terms(a_list, b_list, order, name):
        left = after(tgg, *order)
        return terms(a_list, b_list, ca, left, tgu, pqs, gate_weight, up_weight, aa, name=name)

    a, b = block_terms((2,), (4,), (), "terms_first")
    a2, b4 = a[2], b[4]
    xr, xl = go_x(a2[0], 1), go_x(a2[1], -1)
    zr, zl = go_z(b4[0], 1), go_z(b4[1], -1)

    _, b = block_terms((), (3, 5), a2, "terms_second")
    b3, b5 = b[3], b[5]
    zp = go_z(cat1(b3[0] + zr, b3[1]), 1)
    zm = go_z(cat1(b5[0], b5[1] + zl), -1)

    a, _ = block_terms((1, 3), (), b3, "terms_third")
    a1, a3 = a[1], a[3]
    xp1, xm0 = go_x(a1[1], 1), go_x(a3[0], -1)
    xp0, xm1 = go_x(a1[0] + xr, 1), go_x(a3[1] + xl, -1)

    a, b = block_terms((0,), (2, 6, 1, 7, 0), a1, "terms_fourth")
    b = {k: cat1(*v) for k, v in b.items()}
    zp = go_z(b[2] + zp, 1)
    zm = go_z(b[6] + zm, -1)

    quarter_tokens = tokens // 4
    part = lax.dynamic_slice_in_dim(after(p_t, b[0]), y * quarter_tokens, quarter_tokens, 1)
    px = [go_x(part, d) for d in (2, 1, -1)]
    part = (part + px[0]) + (px[1] + px[2])

    asum = (a[0][0] + xm0 + xp0, a[0][1] + xp1 + xm1)
    rows = asum[0].shape[0] // NZ
    cut = lambda v, k: v[k * rows:(k + 1) * rows]
    t = {k: (cut(asum[0], k), cut(asum[1], k)) for k in range(NZ)}
    ar, al = go_z(t[4][0], 1), go_z(t[4][1], -1)
    zp = go_z(b[1] + zp, 1)
    zm = go_z(b[7] + zm, -1)

    pz = {d: go_z(after(part, ar), d) for d in (1, 2, 3, 4, 5, 6, 7)}
    pair = [part + pz[4], pz[1] + pz[5], pz[2] + pz[6], pz[3] + pz[7]]
    part = (pair[0] + pair[2]) + (pair[1] + pair[3])

    ap = go_z(cat1(t[3][0] + ar, t[3][1]), 1)
    am = go_z(cat1(t[5][0], t[5][1] + al), -1)
    bsum = b[0] + zp + zm
    half = bsum.shape[1] // 2
    quarter = {j: (cut(bsum, j)[:, :half], cut(bsum, j)[:, half:]) for j in range(NX)}
    xr, xl = go_x(quarter[2][0], 1), go_x(quarter[2][1], -1)

    p1, p2, p3 = go_y(part, -1), go_y(part, 2), go_y(part, 1)
    around = cat1(part, p1, p2, p3, part, p1, p2, p3)
    p_full = lax.dynamic_slice_in_dim(around, ((4 - y) % 4) * quarter_tokens, tokens, 1)

    ap = go_z(cat1(*t[2]) + ap, 1)
    am = go_z(cat1(*t[6]) + am, -1)
    xp = go_x(cat1(quarter[1][0] + xr, quarter[1][1]), 1)
    xm = go_x(cat1(quarter[3][0], quarter[3][1] + xl), -1)
    ap = go_z(cat1(*t[1]) + ap, 1)
    am = go_z(cat1(*t[7]) + am, -1)
    right = cat1(*quarter[0]) + xp + xm
    left = cat1(*t[0]) + ap + am
    input_tangent = cat1(left, right)

    hvp_a = lax.dot_general(
        p_full, inputs.astype(F32), (((1,), (0,)), ((), ())),
        preferred_element_type=F32, precision=lax.Precision.HIGHEST,
    )
    hvp_a = hvp_a + swap_core(hvp_a)
    hvp_b = cat0(*factor(place, after(c1, b[0]), up_pre, gu, tgg, tgu, tot))
    hvp_b = hvp_b + swap_core(hvp_b)

    token_count = tokens * lax.axis_size("dp")
    scale_b = math.sqrt(token_count)
    scale_a = math.sqrt(token_count * FF)
    next_a = 2.0 * probe_a.astype(F32) - hvp_a / scale_a
    next_bg = 2.0 * probe_bg.astype(F32) - hvp_b[:16] / scale_b
    next_bu = 2.0 * probe_bu.astype(F32) - hvp_b[16:] / scale_b
    return (input_tangent, next_a, next_bg, next_bu)


def solution(mesh):
    return jax.shard_map(
        shards,
        mesh=mesh,
        in_specs=(
            P("dp", "inp"),
            P("dp", "out"),
            P("dp", "out"),
            P("dp", "out"),
            P("inp", "out"),
            P("inp", "out"),
            P(None, "inp"),
            P(None, "out"),
            P(None, "out"),
            P(None, "inp"),
            P(None, "out"),
            P(None, "out"),
        ),
        out_specs=(P(("dp", "out"), "inp"), P(None, "inp"), P(None, "out"), P(None, "out")),
        check_vma=False,
    )
```

```python
import functools
import math

import jax
import jax.numpy as jnp
from jax import lax
from jax.experimental import pallas as pl
from jax.experimental.pallas import tpu as pltpu
from jax.sharding import PartitionSpec as P

FF = 28672
NX, NZ = 4, 8
F32, BF16 = jnp.float32, jnp.bfloat16
LANES = 128


def dot_nt(left, right):
    return lax.dot_general(left, right, (((1,), (1,)), ((), ())), preferred_element_type=F32)


def dot_nn(left, right):
    return lax.dot_general(left, right, (((1,), (0,)), ((), ())), preferred_element_type=F32)


def dot_tn(left, right):
    return lax.dot_general(left, right, (((0,), (0,)), ((), ())), preferred_element_type=F32)


def split2(value):
    high = value.astype(BF16)
    return high, (value - high.astype(F32)).astype(BF16)


def split3(value):
    high = value.astype(BF16)
    rest = value - high.astype(F32)
    mid = rest.astype(BF16)
    return high, mid, (rest - mid.astype(F32)).astype(BF16)


def params(mib=26):
    return pltpu.CompilerParams(vmem_limit_bytes=mib * 1024 * 1024)


VMEM = pl.BlockSpec(memory_space=pltpu.VMEM)
SMEM = pl.BlockSpec(memory_space=pltpu.SMEM)
COST = pl.CostEstimate(flops=1000, bytes_accessed=1000, transcendentals=0)


def elementwise(g, u, dy):
    g, u, dy = g.astype(F32), u.astype(F32), dy.astype(F32)
    sig = 1.0 / (1.0 + jnp.exp(-g))
    rest = 1.0 - sig
    s = g * sig
    c1 = dy * (sig + s * rest)
    c2 = dy * u * (rest * (2.0 * sig + s - 2.0 * s * sig))
    return c1, c2, c1 * u, dy * s


def rank_terms(gg, gu, rg, ru):
    gg_hi, gg_lo = split2(gg)
    gu_hi, gu_lo = split2(gu)
    return (dot_nt(gg_hi, rg) + dot_nt(gg_lo, rg)) + (dot_nt(gu_hi, ru) + dot_nt(gu_lo, ru))


def tangent_math(both, c1, c2, pq, rpg, rpu):
    width = c1.shape[1]
    tang_g, tang_u = both[:, :width], both[:, width:]
    tgg = (tang_u * c1 + c2 * tang_g).astype(BF16)
    tgu = (c1 * tang_g).astype(BF16)
    pq = pq + (dot_nt(tgg, rpg) + dot_nt(tgu, rpu))
    high = pq.astype(BF16).astype(F32)
    return tgg, tgu, pq, (high + pltpu.roll(pq - high, 32, 1)).astype(BF16)


def body_kernel(place, g_ref, u_ref, dy_ref, tot_ref, bst_ref, rg_ref, ru_ref, rpg_ref, rpu_ref,
                tgg_ref, tgu_ref, pqs_ref, pt_ref, hg_ref, hu_ref):
    c1, c2, gg, gu = elementwise(g_ref[...], u_ref[...], dy_ref[...])
    tot = tot_ref[...]
    both = dot_tn(jnp.concatenate(split3(tot), axis=0), bst_ref[...])
    tgg, tgu, pq, full = tangent_math(
        both, c1, c2, rank_terms(gg, gu, rg_ref[...], ru_ref[...]), rpg_ref[...], rpu_ref[...]
    )
    pt_ref[...] = pq[:, :16].T
    rows = tgg.shape[0] // NX
    for xx in range(NX):
        j = lax.rem(xx - place[1] + NX, NX)
        part = slice(xx * rows, (xx + 1) * rows)
        tgg_ref[0, j] = tgg[part]
        tgu_ref[0, j] = tgu[part]
        pqs_ref[0, j] = full[part]

    t_hi, t_lo = split2(tot)
    xv = jnp.concatenate([t_hi[:16], t_lo[:16]], axis=0)
    xa = jnp.concatenate([t_hi[16:], t_lo[16:]], axis=0)

    def both_terms(grad, tan):
        hi, lo = split2(grad)
        sums = dot_nn(xv, hi) + dot_nn(xa, tan)
        return sums[:16] + sums[16:] + dot_nn(xv[:16], lo)

    hg, hu = both_terms(gg, tgg), both_terms(gu, tgu)
    first = pl.program_id(0) == 0

    @pl.when(first)
    def _():
        hg_ref[...] = hg
        hu_ref[...] = hu

    @pl.when(jnp.logical_not(first))
    def _():
        hg_ref[...] += hg
        hu_ref[...] += hu


def body(place, g, u, dy, tot, bst, rg, ru, rpg, rpu):
    tokens, width = g.shape
    block = tokens // NZ
    rows = block // NX

    def nat(k, s):
        return lax.rem(k + s[0], NZ)

    row = pl.BlockSpec((block, width), lambda k, s: (nat(k, s), 0))
    rel = lambda n: pl.BlockSpec((1, NX, rows, n), lambda k, s: (k, 0, 0, 0))
    fixed = lambda a: pl.BlockSpec(a.shape, lambda k, s: (0, 0))
    rank = pl.BlockSpec((16, width), lambda k, s: (0, 0))
    return pl.pallas_call(
        body_kernel,
        grid_spec=pltpu.PrefetchScalarGridSpec(
            num_scalar_prefetch=1,
            grid=(NZ,),
            in_specs=[
                row, row, row,
                pl.BlockSpec((32, block), lambda k, s: (0, nat(k, s))),
                fixed(bst), fixed(rg), fixed(ru), fixed(rpg), fixed(rpu),
            ],
            out_specs=[
                rel(width), rel(width), rel(LANES),
                pl.BlockSpec((16, block), lambda k, s: (0, nat(k, s))),
                rank, rank,
            ],
        ),
        out_shape=[
            jax.ShapeDtypeStruct((NZ, NX, rows, width), BF16),
            jax.ShapeDtypeStruct((NZ, NX, rows, width), BF16),
            jax.ShapeDtypeStruct((NZ, NX, rows, LANES), BF16),
            jax.ShapeDtypeStruct((16, tokens), F32),
            jax.ShapeDtypeStruct((16, width), F32),
            jax.ShapeDtypeStruct((16, width), F32),
        ],
        compiler_params=params(20),
        cost_estimate=COST,
        name="body",
    )(place, g, u, dy, tot, bst, rg, ru, rpg, rpu)


def terms_kernel(a_list, b_list, ca, tgg_ref, tgu_ref, pqs_ref, gw_ref, uw_ref, aa_ref, *outs):
    def rows_of(ref, index):
        value = ref[index]
        return value.reshape(-1, ref.shape[-1])

    def one(indices, low, high, out_refs):
        def left(ref):
            got = [rows_of(ref, i) for i in indices]
            return got[0] if len(got) == 1 else jnp.concatenate(got, axis=0)

        lg, lu, lp = left(tgg_ref), left(tgu_ref), left(pqs_ref)
        step = 256
        n = lg.shape[0] // len(indices)
        for c in range(low, high, step):
            cols = slice(c, c + step)
            value = (dot_nt(lg, gw_ref[cols]) + dot_nt(lu, uw_ref[cols])) + dot_nt(lp, aa_ref[cols])
            for m, refs in enumerate(out_refs):
                off = c - low
                for ref in refs:
                    if off < ref.shape[1]:
                        ref[:, off:off + step] = value[m * n:(m + 1) * n]
                        break
                    off -= ref.shape[1]

    outs = list(outs)
    a_outs = [[outs.pop(0), outs.pop(0)] for _ in a_list]
    b_outs = [[outs.pop(0), outs.pop(0)] for _ in b_list]
    if a_list:
        one([(slice(None), j) for j in a_list], 0, ca, a_outs)
    if b_list:
        one([(k,) for k in b_list], ca, gw_ref.shape[0], b_outs)


def terms(a_list, b_list, ca, tgg, tgu, pqs, gw, uw, aa, name):
    nz, nx, rows, _ = tgg.shape
    cb = gw.shape[0] - ca
    shapes = []
    for _ in a_list:
        shapes += [jax.ShapeDtypeStruct((nz * rows, ca // 2), F32)] * 2
    for _ in b_list:
        shapes += [jax.ShapeDtypeStruct((nx * rows, cb // 2), F32)] * 2
    vm = pl.BlockSpec(memory_space=pltpu.VMEM)
    share = len(a_list) / 8 + len(b_list) / 16
    outs = pl.pallas_call(
        functools.partial(terms_kernel, a_list, b_list, ca),
        in_specs=[vm] * 6,
        out_specs=[vm] * len(shapes),
        out_shape=shapes,
        compiler_params=params(),
        cost_estimate=COST,
        name=name,
    )(tgg, tgu, pqs, gw, uw, aa)
    outs = list(outs)
    a = {j: (outs.pop(0), outs.pop(0)) for j in a_list}
    b = {k: (outs.pop(0), outs.pop(0)) for k in b_list}
    return a, b


def block_at(place, block):
    return lax.rem(place[0] + block[0], NZ), lax.rem(place[1] + block[1], NX)


def ahead_early_kernel(blocks, place, g_ref, u_ref, dy_ref, bg_ref, bu_ref, pg_ref, pu_ref,
                       c1_ref, c2_ref, pq_ref, rg, ru):
    for ref, first, second in ((rg, pg_ref, bg_ref), (ru, pu_ref, bu_ref)):
        ref[...] = jnp.zeros_like(ref)
        ref[0:16] = first[...]
        ref[16:32] = second[...]
    rows = g_ref.shape[2]
    group = 4
    for n in range(0, len(blocks), group):
        at = [block_at(place, block) for block in blocks[n:n + group]]
        value = lambda ref: jnp.concatenate([ref[z, x] for z, x in at], axis=0)
        c1, c2, gg, gu = elementwise(value(g_ref), value(u_ref), value(dy_ref))
        part = slice(n * rows, (n + group) * rows)
        c1_ref[part] = c1
        c2_ref[part] = c2
        pq_ref[part] = rank_terms(gg, gu, rg[...], ru[...])


def ahead_early(blocks, place, g, u, dy, factors, name):
    rows, width = g.shape[2:]
    wide = jax.ShapeDtypeStruct((len(blocks) * rows, width), F32)
    return pl.pallas_call(
        functools.partial(ahead_early_kernel, blocks),
        in_specs=[SMEM] + [VMEM] * 7,
        out_specs=[VMEM] * 3,
        out_shape=[wide, wide, jax.ShapeDtypeStruct((len(blocks) * rows, LANES), F32)],
        scratch_shapes=[pltpu.VMEM((LANES, width), BF16), pltpu.VMEM((LANES, width), BF16)],
        compiler_params=params(20),
        cost_estimate=COST,
        name=name,
    )(place, g, u, dy, *factors)


def ahead_kernel(blocks, groups, place, c1_ref, c2_ref, pq_ref, tot_ref, bg_ref, bu_ref, pg_ref, pu_ref,
                 gw_ref, uw_ref, a_ref, pa_ref, *rest):
    outs, (tot_rows, bst, rp, aa) = rest[:-4], rest[-4:]
    width = c1_ref.shape[1]
    rows = tot_rows.shape[1]
    tot_rows[...] = tot_ref[...].T.reshape(tot_rows.shape)
    for n in range(0, 96, 32):
        bst[n:n + 16, :width] = bg_ref[...]
        bst[n:n + 16, width:] = bu_ref[...]
        bst[n + 16:n + 32, :width] = pg_ref[...]
        bst[n + 16:n + 32, width:] = pu_ref[...]
    rp[...] = jnp.zeros_like(rp)
    rp[0, 0:16] = bg_ref[...]
    rp[1, 0:16] = bu_ref[...]
    aa[...] = jnp.zeros_like(aa)
    for n in (0, 32):
        aa[n:n + 16] = a_ref[...]
        aa[n + 16:n + 32] = pa_ref[...]
    at = [block_at(place, block) for block in blocks]
    tot = jnp.concatenate([tot_rows[z * NX + x] for z, x in at], axis=0)
    both = dot_nn(jnp.concatenate(split3(tot), axis=1), bst[...])
    tgg, tgu, _, full = tangent_math(both, c1_ref[...], c2_ref[...], pq_ref[...], rp[0], rp[1])
    step = 256
    for g, (start, count, low) in enumerate(groups):
        part = slice(start * rows, (start + count) * rows)
        for i in range(2):
            ref = outs[2 * g + i]
            for c in range(0, ref.shape[1], step):
                first = low + i * ref.shape[1] + c
                cols = slice(first, first + step)
                ref[:, c:c + step] = (
                    dot_nt(tgg[part], gw_ref[cols]) + dot_nt(tgu[part], uw_ref[cols])
                ) + dot_nn(full[part], aa[:, cols])


def ahead(blocks, groups, place, early, tot, factors, gw, uw, a, pa, ca, name):
    rows = early[0].shape[0] // len(blocks)
    width = early[0].shape[1]
    model = gw.shape[0]
    shapes = []
    for _, count, low in groups:
        columns = model - ca if low else ca
        shapes += [jax.ShapeDtypeStruct((count * rows, columns // 2), F32)] * 2
    outs = pl.pallas_call(
        functools.partial(ahead_kernel, blocks, groups),
        in_specs=[SMEM] + [VMEM] * 12,
        out_specs=[VMEM] * len(shapes),
        out_shape=shapes,
        scratch_shapes=[
            pltpu.VMEM((NZ * NX, rows, 32), F32),
            pltpu.VMEM((96, 2 * width), BF16),
            pltpu.VMEM((2, LANES, width), BF16),
            pltpu.VMEM((LANES, model), BF16),
        ],
        compiler_params=params(28),
        cost_estimate=COST,
        name=name,
    )(place, *early, tot, *factors, gw, uw, a, pa)
    return [tuple(outs[2 * g:2 * g + 2]) for g in range(len(groups))]


def out_perm(dz, dx):
    return [(z * NX + x, ((z + dz) % NZ) * NX + (x + dx) % NX) for z in range(NZ) for x in range(NX)]


def go_x(value, d):
    return lax.ppermute(value, "out", out_perm(0, d))


def go_z(value, d):
    return lax.ppermute(value, "out", out_perm(d, 0))


def go_y(value, d):
    return lax.ppermute(value, "inp", [(i, (i + d) % 4) for i in range(4)])


def pair_x(value, mask):
    return lax.ppermute(value, "out", [(z * NX + x, z * NX + (x ^ mask)) for z in range(NZ) for x in range(NX)])


def pair_z(value, mask):
    return lax.ppermute(value, "out", [(z * NX + x, (z ^ mask) * NX + x) for z in range(NZ) for x in range(NX)])


def swap_core(value):
    return lax.ppermute(value, "dp", [(0, 1), (1, 0)])


def after(value, *others):
    return lax.optimization_barrier((value,) + others)[0]


def shards(inputs, gate_pre, up_pre, upstream, gate_weight, up_weight,
           a_down, b_gate, b_up, probe_a, probe_bg, probe_bu):
    tokens = inputs.shape[0]
    ca = gate_weight.shape[0] // 2
    place_out = lax.axis_index("out")
    place = jnp.stack([place_out // NX, place_out % NX]).astype(jnp.int32)
    y = lax.axis_index("inp")
    cat0 = lambda *a: jnp.concatenate(a, axis=0)
    cat1 = lambda *a: jnp.concatenate(a, axis=1)
    lanes0 = lambda v: jnp.pad(v, ((0, LANES - v.shape[0]), (0, 0)))

    local = dot_nt(cat0(probe_a, a_down), inputs)
    across, ahead_y, behind = go_y(local, 2), go_y(local, 1), go_y(local, -1)

    factors = (b_gate, b_up, probe_bg, probe_bu)
    rows = tokens // (NZ * NX)
    raw = [v.reshape(NZ, NX, rows, v.shape[1]) for v in (gate_pre, up_pre, upstream)]
    blocks0 = [(k, 2) for k in range(NZ)] + [(4, j) for j in range(NX)]
    blocks1 = [(k, j) for k in (3, 5) for j in range(NX)]
    blocks2 = [(k, j) for j in (1, 3) for k in range(NZ)]
    early0 = ahead_early(blocks0, place, *raw, factors, "early_first")
    early1 = ahead_early(blocks1, place, after(raw[0], early0[0]), *raw[1:], factors, "early_second")
    early2 = ahead_early(blocks2, place, after(raw[0], early1[0]), *raw[1:], factors, "early_third")

    tot = (after(local, early2[0]) + across) + (ahead_y + behind)
    weights = (gate_weight, up_weight, a_down, probe_a)
    a2, b4 = ahead(blocks0, ((0, 8, 0), (8, 4, ca)), place, early0, tot, factors, *weights, ca, "send_first")
    xr, xl = go_x(a2[0], 1), go_x(a2[1], -1)
    zr, zl = go_z(b4[0], 1), go_z(b4[1], -1)

    tot1 = after(tot, *a2)
    b3, b5 = ahead(blocks1, ((0, 4, ca), (4, 4, ca)), place, early1, tot1, factors, *weights, ca, "send_second")
    tot2 = after(tot, *b3)
    a1, a3 = ahead(blocks2, ((0, 8, 0), (8, 8, 0)), place, early2, tot2, factors, *weights, ca, "send_third")

    sp = cat1(after(b3[0], a1[0]) + zr, b3[1])
    sm = cat1(after(b5[0], a1[0]), b5[1] + zl)
    zp, zm = go_z(sp, 1), go_z(sm, -1)

    small = cat1(cat0(b_gate, probe_bg), cat0(b_up, probe_bu))
    tgg, tgu, pqs, p_t, hvp_bg, hvp_bu = body(
        place, gate_pre, up_pre, upstream, after(tot, sp, sm), cat0(small, small, small),
        lanes0(cat0(probe_bg, b_gate)), lanes0(cat0(probe_bu, b_up)), lanes0(b_gate), lanes0(b_up),
    )

    tp, tm = cat1(after(a1[0], tgg) + xr, a1[1]), cat1(a3[0], a3[1] + xl)
    xp, xm = go_x(tp, 1), go_x(tm, -1)

    aa = lanes0(cat0(a_down, probe_a, a_down, probe_a)).T
    a, b = terms(
        (0,), (2, 6, 1, 7, 0), ca, after(tgg, tp, tm), tgu, pqs, gate_weight, up_weight, aa, name="terms_rest"
    )
    b = {k: cat1(*v) for k, v in b.items()}

    quarter_tokens = tokens // 4
    part = lax.dynamic_slice_in_dim(after(p_t, b[0]), y * quarter_tokens, quarter_tokens, 1)
    part = part + pair_x(part, 1)

    sp, sm = b[2] + zp, b[6] + zm
    zp, zm = go_z(sp, 1), go_z(sm, -1)
    part = after(part, sp, sm)
    part = part + pair_x(part, 3)
    part = part + pair_z(part, 1)
    hvp_b = after(cat0(hvp_bg, hvp_bu), part)
    hvp_b = hvp_b + swap_core(hvp_b)

    sp, sm = b[1] + zp, b[7] + zm
    zp, zm = go_z(sp, 1), go_z(sm, -1)
    part = after(part, sp, sm)
    part = part + pair_z(part, 2)

    middle = a[0][0].shape[1]
    asum = (a[0][0] + xp[:, :middle] + xm[:, :middle], a[0][1] + xp[:, middle:] + xm[:, middle:])
    cut = lambda v, k: v[k * rows:(k + 1) * rows]
    t = {k: (cut(asum[0], k), cut(asum[1], k)) for k in range(NZ)}
    ar, al = go_z(t[4][0], 1), go_z(t[4][1], -1)

    part = after(part, *asum)
    part = part + pair_z(part, 4)

    sp, sm = cat1(t[3][0] + ar, t[3][1]), cat1(t[5][0], t[5][1] + al)
    ap, am = go_z(sp, 1), go_z(sm, -1)

    part = after(part, sp, sm)
    p1, p2, p3 = go_y(part, -1), go_y(part, 2), go_y(part, 1)
    around = cat1(part, p1, p2, p3, part, p1, p2, p3)
    p_full = lax.dynamic_slice_in_dim(around, ((4 - y) % 4) * quarter_tokens, tokens, 1)

    bsum = b[0] + zp + zm
    half = bsum.shape[1] // 2
    quarter = {j: (cut(bsum, j)[:, :half], cut(bsum, j)[:, half:]) for j in range(NX)}
    xr, xl = go_x(quarter[2][0], 1), go_x(quarter[2][1], -1)

    sp, sm = cat1(*t[2]) + ap, cat1(*t[6]) + am
    ap, am = go_z(sp, 1), go_z(sm, -1)
    xp = go_x(cat1(quarter[1][0] + xr, quarter[1][1]), 1)
    xm = go_x(cat1(quarter[3][0], quarter[3][1] + xl), -1)
    ap = go_z(cat1(*t[1]) + ap, 1)
    am = go_z(cat1(*t[7]) + am, -1)
    right = cat1(*quarter[0]) + xp + xm
    left = cat1(*t[0]) + ap + am
    input_tangent = cat1(left, right)

    hvp_a = lax.dot_general(
        p_full, inputs.astype(F32), (((1,), (0,)), ((), ())),
        preferred_element_type=F32, precision=lax.Precision.HIGHEST,
    )
    hvp_a = hvp_a + swap_core(hvp_a)

    token_count = tokens * lax.axis_size("dp")
    scale_b = math.sqrt(token_count)
    scale_a = math.sqrt(token_count * FF)
    next_a = 2.0 * probe_a.astype(F32) - hvp_a / scale_a
    next_bg = 2.0 * probe_bg.astype(F32) - hvp_b[:16] / scale_b
    next_bu = 2.0 * probe_bu.astype(F32) - hvp_b[16:] / scale_b
    return (input_tangent, next_a, next_bg, next_bu)


def solution(mesh):
    return jax.shard_map(
        shards,
        mesh=mesh,
        in_specs=(
            P("dp", "inp"),
            P("dp", "out"),
            P("dp", "out"),
            P("dp", "out"),
            P("inp", "out"),
            P("inp", "out"),
            P(None, "inp"),
            P(None, "out"),
            P(None, "out"),
            P(None, "inp"),
            P(None, "out"),
            P(None, "out"),
        ),
        out_specs=(P(("dp", "out"), "inp"), P(None, "inp"), P(None, "out"), P(None, "out")),
        check_vma=False,
    )
```

```python
import functools
import math

import jax
import jax.numpy as jnp
from jax import lax
from jax.experimental import pallas as pl
from jax.experimental.pallas import tpu as pltpu
from jax.sharding import PartitionSpec as P

FF = 28672
NX, NZ = 4, 8
F32, BF16 = jnp.float32, jnp.bfloat16
LANES = 128


def dot_nt(left, right):
    return lax.dot_general(left, right, (((1,), (1,)), ((), ())), preferred_element_type=F32)


def dot_nn(left, right):
    return lax.dot_general(left, right, (((1,), (0,)), ((), ())), preferred_element_type=F32)


def dot_tn(left, right):
    return lax.dot_general(left, right, (((0,), (0,)), ((), ())), preferred_element_type=F32)


def split2(value):
    high = value.astype(BF16)
    return high, (value - high.astype(F32)).astype(BF16)


def split3(value):
    high = value.astype(BF16)
    rest = value - high.astype(F32)
    mid = rest.astype(BF16)
    return high, mid, (rest - mid.astype(F32)).astype(BF16)


def params(mib=26):
    return pltpu.CompilerParams(vmem_limit_bytes=mib * 1024 * 1024)


VMEM = pl.BlockSpec(memory_space=pltpu.VMEM)
SMEM = pl.BlockSpec(memory_space=pltpu.SMEM)
COST = pl.CostEstimate(flops=1000, bytes_accessed=1000, transcendentals=0)
LONG = pl.CostEstimate(flops=24_000_000_000, bytes_accessed=90_000_000, transcendentals=0)


def early_tables(rg, ru, bg_ref, bu_ref, pg_ref, pu_ref):
    for ref, first, second in ((rg, pg_ref, bg_ref), (ru, pu_ref, bu_ref)):
        ref[...] = jnp.zeros_like(ref)
        ref[0:16] = first[...]
        ref[16:32] = second[...]


def tangent_tables(bst, rp, bg_ref, bu_ref, pg_ref, pu_ref):
    width = bg_ref.shape[1]
    for n in range(0, 96, 32):
        bst[n:n + 16, :width] = bg_ref[...]
        bst[n:n + 16, width:] = bu_ref[...]
        bst[n + 16:n + 32, :width] = pg_ref[...]
        bst[n + 16:n + 32, width:] = pu_ref[...]
    rp[...] = jnp.zeros_like(rp)
    rp[0, 0:16] = bg_ref[...]
    rp[1, 0:16] = bu_ref[...]


def rank_table(aa, a_ref, pa_ref):
    aa[...] = jnp.zeros_like(aa)
    for n in (0, 32):
        aa[n:n + 16] = a_ref[...]
        aa[n + 16:n + 32] = pa_ref[...]


def elementwise(g, u, dy):
    g, u, dy = g.astype(F32), u.astype(F32), dy.astype(F32)
    sig = 1.0 / (1.0 + jnp.exp(-g))
    rest = 1.0 - sig
    s = g * sig
    c1 = dy * (sig + s * rest)
    c2 = dy * u * (rest * (2.0 * sig + s - 2.0 * s * sig))
    return c1, c2, c1 * u, dy * s


def rank_terms(gg, gu, rg, ru):
    gg_hi, gg_lo = split2(gg)
    gu_hi, gu_lo = split2(gu)
    return (dot_nt(gg_hi, rg) + dot_nt(gg_lo, rg)) + (dot_nt(gu_hi, ru) + dot_nt(gu_lo, ru))


def tangent_math(both, c1, c2, pq, rpg, rpu):
    width = c1.shape[1]
    tang_g, tang_u = both[:, :width], both[:, width:]
    tgg = (tang_u * c1 + c2 * tang_g).astype(BF16)
    tgu = (c1 * tang_g).astype(BF16)
    pq = pq + (dot_nt(tgg, rpg) + dot_nt(tgu, rpu))
    high = pq.astype(BF16).astype(F32)
    return tgg, tgu, pq, (high + pltpu.roll(pq - high, 32, 1)).astype(BF16)


def body_kernel(place, c1_ref, c2_ref, gu_ref, pq_ref, u_ref, tot_ref, bg_ref, bu_ref, pg_ref, pu_ref,
                tgg_ref, tgu_ref, pqs_ref, hg_ref, hu_ref, bst, rp):
    first = pl.program_id(0) == 0

    @pl.when(first)
    def _():
        tangent_tables(bst, rp, bg_ref, bu_ref, pg_ref, pu_ref)

    c1 = c1_ref[...]
    tot = tot_ref[...]
    both = dot_tn(jnp.concatenate(split3(tot), axis=0), bst[...])
    tgg, tgu, _, full = tangent_math(both, c1, c2_ref[...], pq_ref[...], rp[0], rp[1])
    rows = tgg.shape[0] // NX
    for xx in range(NX):
        j = lax.rem(xx - place[1] + NX, NX)
        part = slice(xx * rows, (xx + 1) * rows)
        tgg_ref[0, j] = tgg[part]
        tgu_ref[0, j] = tgu[part]
        pqs_ref[0, j] = full[part]

    t_hi, t_lo = split2(tot)
    xv = jnp.concatenate([t_hi[:16], t_lo[:16]], axis=0)
    xa = jnp.concatenate([t_hi[16:], t_lo[16:]], axis=0)

    def both_terms(grad, tan):
        hi, lo = split2(grad)
        sums = dot_nn(xv, hi) + dot_nn(xa, tan)
        return sums[:16] + sums[16:] + dot_nn(xv[:16], lo)

    hg = both_terms(c1 * u_ref[...].astype(F32), tgg)
    hu = both_terms(gu_ref[...], tgu)

    @pl.when(first)
    def _():
        hg_ref[...] = hg
        hu_ref[...] = hu

    @pl.when(jnp.logical_not(first))
    def _():
        hg_ref[...] += hg
        hu_ref[...] += hu


def body(order, place, c1, c2, gu, pq, u, tot, factors, name, cost=COST):
    tokens, width = u.shape
    block = tokens // NZ
    rows = block // NX

    def nat(i, s):
        k = order[-1]
        for n, value in enumerate(order[:-1]):
            k = jnp.where(i == n, value, k)
        return lax.rem(k + s[0], NZ)

    row = pl.BlockSpec((block, width), lambda i, s: (nat(i, s), 0))
    rel = lambda n: pl.BlockSpec((1, NX, rows, n), lambda i, s: (i, 0, 0, 0))
    rank = pl.BlockSpec((16, width), lambda i, s: (0, 0))
    return pl.pallas_call(
        body_kernel,
        grid_spec=pltpu.PrefetchScalarGridSpec(
            num_scalar_prefetch=1,
            grid=(len(order),),
            in_specs=[
                row, row, row,
                pl.BlockSpec((block, LANES), lambda i, s: (nat(i, s), 0)),
                row,
                pl.BlockSpec((32, block), lambda i, s: (0, nat(i, s))),
                rank, rank, rank, rank,
            ],
            out_specs=[rel(width), rel(width), rel(LANES), rank, rank],
            scratch_shapes=[pltpu.VMEM((96, 2 * width), BF16), pltpu.VMEM((2, LANES, width), BF16)],
        ),
        out_shape=[
            jax.ShapeDtypeStruct((len(order), NX, rows, width), BF16),
            jax.ShapeDtypeStruct((len(order), NX, rows, width), BF16),
            jax.ShapeDtypeStruct((len(order), NX, rows, LANES), BF16),
            jax.ShapeDtypeStruct((16, width), F32),
            jax.ShapeDtypeStruct((16, width), F32),
        ],
        compiler_params=params(20),
        cost_estimate=cost,
        name=name,
    )(place, c1, c2, gu, pq, u, tot, *factors)


def terms_kernel(sources, jobs, gw_ref, uw_ref, a_ref, pa_ref, *rest):
    ins, outs, aa = rest[:3 * sources], rest[3 * sources:-1], rest[-1]
    rank_table(aa, a_ref, pa_ref)
    step = 256
    done = 0
    for blocks, low, columns, parts in jobs:
        def left(which):
            got = [ins[3 * source + which][index].reshape(-1, ins[3 * source + which].shape[-1])
                   for source, index in blocks]
            return got[0] if len(got) == 1 else jnp.concatenate(got, axis=0)

        lg, lu, lp = left(0), left(1), left(2)
        n = lg.shape[0] // parts
        for c in range(0, columns, step):
            cols = slice(low + c, low + c + step)
            value = (dot_nt(lg, gw_ref[cols]) + dot_nt(lu, uw_ref[cols])) + dot_nn(lp, aa[:, cols])
            for m in range(parts):
                outs[done + m][:, c:c + step] = value[m * n:(m + 1) * n]
        done += parts


def terms(bodies, jobs, gw, uw, a_down, probe_a, name):
    nx, rows = bodies[0][0].shape[1:3]
    shapes = []
    for blocks, _, columns, parts in jobs:
        count = sum(bodies[source][0][index].size for source, index in blocks) // bodies[0][0].shape[-1]
        shapes += [jax.ShapeDtypeStruct((count // parts, columns), F32)] * parts
    flat = [v for three in bodies for v in three]
    return pl.pallas_call(
        functools.partial(terms_kernel, len(bodies), jobs),
        in_specs=[VMEM] * (4 + len(flat)),
        out_specs=[VMEM] * len(shapes),
        out_shape=shapes,
        scratch_shapes=[pltpu.VMEM((LANES, gw.shape[0]), BF16)],
        compiler_params=params(18),
        cost_estimate=COST,
        name=name,
    )(gw, uw, a_down, probe_a, *flat)


def early_kernel(g_ref, u_ref, dy_ref, bg_ref, bu_ref, pg_ref, pu_ref, c1_ref, c2_ref, gu_ref, pq_ref, rg, ru):
    early_tables(rg, ru, bg_ref, bu_ref, pg_ref, pu_ref)
    block = g_ref.shape[0] // 8
    for n in range(8):
        rows = slice(n * block, (n + 1) * block)
        c1, c2, gg, gu = elementwise(g_ref[rows], u_ref[rows], dy_ref[rows])
        c1_ref[rows] = c1
        c2_ref[rows] = c2
        gu_ref[rows] = gu
        pq_ref[rows] = rank_terms(gg, gu, rg[...], ru[...])


def early(g, u, dy, factors):
    tokens, width = g.shape
    wide = jax.ShapeDtypeStruct((tokens, width), F32)
    return pl.pallas_call(
        early_kernel,
        in_specs=[VMEM] * 7,
        out_specs=[VMEM] * 4,
        out_shape=[wide, wide, wide, jax.ShapeDtypeStruct((tokens, LANES), F32)],
        scratch_shapes=[pltpu.VMEM((LANES, width), BF16), pltpu.VMEM((LANES, width), BF16)],
        compiler_params=params(22),
        cost_estimate=COST,
        name="early",
    )(g, u, dy, *factors)


def block_at(place, block):
    if len(block) == 3:
        return 2 * place[2] + block[1], block[2]
    return lax.rem(place[0] + block[0], NZ), lax.rem(place[1] + block[1], NX)


def ahead_kernel(blocks, groups, rank_blocks, place, c1_ref, c2_ref, pq_ref, tot_ref, bg_ref, bu_ref,
                 pg_ref, pu_ref, gw_ref, uw_ref, a_ref, pa_ref, *rest):
    outs, (tot_rows, bst, rp, aa) = rest[:-4], rest[-4:]
    rows = tot_rows.shape[1]
    tot_rows[...] = tot_ref[...].T.reshape(tot_rows.shape)
    tangent_tables(bst, rp, bg_ref, bu_ref, pg_ref, pu_ref)
    rank_table(aa, a_ref, pa_ref)
    at = [block_at(place, block) for block in blocks]
    gather = lambda ref: jnp.concatenate([ref[z, x] for z, x in at], axis=0)
    tot = jnp.concatenate([tot_rows[z * NX + x] for z, x in at], axis=0)
    both = dot_nn(jnp.concatenate(split3(tot), axis=1), bst[...])
    tgg, tgu, pq, full = tangent_math(both, gather(c1_ref), gather(c2_ref), gather(pq_ref), rp[0], rp[1])
    if rank_blocks is not None:
        low = rank_blocks * rows
        for n in range(0, pq.shape[0] - low, LANES):
            turned = pq[low + n:low + n + LANES].T
            for ref in outs[:2]:
                ref[-8:, n:n + LANES] = turned[0:8]
                ref[-8:, 256 + n:256 + n + LANES] = turned[8:16]
    step = 256
    for g, (start, count, low) in enumerate(groups):
        part = slice(start * rows, (start + count) * rows)
        for i in range(2):
            ref = outs[2 * g + i]
            for c in range(0, ref.shape[1], step):
                first = low + i * ref.shape[1] + c
                cols = slice(first, first + step)
                ref[:count * rows, c:c + step] = (
                    dot_nt(tgg[part], gw_ref[cols]) + dot_nt(tgu[part], uw_ref[cols])
                ) + dot_nn(full[part], aa[:, cols])


def ahead(blocks, groups, place, early_out, tot, factors, gw, uw, a, pa, ca, name, rank_blocks=None):
    rows, width = early_out[0].shape[2:]
    model = gw.shape[0]
    shapes = []
    for g, (_, count, low) in enumerate(groups):
        columns = model - ca if low else ca
        more = 8 if g == 0 and rank_blocks is not None else 0
        shapes += [jax.ShapeDtypeStruct((count * rows + more, columns // 2), F32)] * 2
    outs = pl.pallas_call(
        functools.partial(ahead_kernel, blocks, groups, rank_blocks),
        in_specs=[SMEM] + [VMEM] * 12,
        out_specs=[VMEM] * len(shapes),
        out_shape=shapes,
        scratch_shapes=[
            pltpu.VMEM((NZ * NX, rows, 32), F32),
            pltpu.VMEM((96, 2 * width), BF16),
            pltpu.VMEM((2, LANES, width), BF16),
            pltpu.VMEM((LANES, model), BF16),
        ],
        compiler_params=params(20),
        cost_estimate=COST,
        name=name,
    )(place, *early_out, tot, *factors, gw, uw, a, pa)
    return [tuple(outs[2 * g:2 * g + 2]) for g in range(len(groups))]


def width_kernel(place, p0_ref, p1_ref, p2_ref, p3_ref, x_ref, out_ref):
    quarter = p0_ref.shape[1] // 2
    total = None
    for n, ref in enumerate((p0_ref, p1_ref, p2_ref, p3_ref)):
        start = pl.multiple_of(lax.rem(place[2] + n, 4) * quarter, quarter)
        p = jnp.concatenate([ref[:, :quarter], ref[:, quarter:]], axis=0)
        part = dot_nn(jnp.concatenate(split3(p), axis=0), x_ref[pl.ds(start, quarter), :])
        part = part[:16] + (part[16:32] + part[32:])
        total = part if total is None else total + part
    out_ref[...] = total


def width_sum(place, quarters, inputs):
    return pl.pallas_call(
        width_kernel,
        in_specs=[SMEM] + [VMEM] * 5,
        out_specs=VMEM,
        out_shape=jax.ShapeDtypeStruct((16, inputs.shape[1]), F32),
        compiler_params=params(12),
        cost_estimate=COST,
        name="width_sum",
    )(place, *quarters, inputs)


def place_kernel(place_ref, out_ref):
    for n in range(3):
        out_ref[n] = place_ref[n]


def hand_on(place):
    return pl.pallas_call(
        place_kernel,
        in_specs=[SMEM],
        out_specs=SMEM,
        out_shape=jax.ShapeDtypeStruct((3,), jnp.int32),
        cost_estimate=LONG,
        name="hand_on",
    )(place)


def out_perm(dz, dx):
    return [(z * NX + x, ((z + dz) % NZ) * NX + (x + dx) % NX) for z in range(NZ) for x in range(NX)]


def go_x(value, d):
    return lax.ppermute(value, "out", out_perm(0, d))


def go_z(value, d):
    return lax.ppermute(value, "out", out_perm(d, 0))


def go_y(value, d):
    return lax.ppermute(value, "inp", [(i, (i + d) % 4) for i in range(4)])


def pair_x(value, mask):
    return lax.ppermute(value, "out", [(z * NX + x, z * NX + (x ^ mask)) for z in range(NZ) for x in range(NX)])


def pair_z(value, mask):
    return lax.ppermute(value, "out", [(z * NX + x, (z ^ mask) * NX + x) for z in range(NZ) for x in range(NX)])


def swap_core(value):
    return lax.ppermute(value, "dp", [(0, 1), (1, 0)])


def send(go, ahead_value, back_value):
    return go(ahead_value, 1), go(back_value, -1)


def together(*values):
    return lax.optimization_barrier(values)


def after(value, *others):
    return lax.optimization_barrier((value,) + others)[0]


def shards(inputs, gate_pre, up_pre, upstream, gate_weight, up_weight,
           a_down, b_gate, b_up, probe_a, probe_bg, probe_bu):
    tokens = inputs.shape[0]
    ca = gate_weight.shape[0] // 2
    at = lax.axis_index("out")
    place = jnp.stack([at >> 2, at & 3, lax.axis_index("inp")]).astype(jnp.int32)
    place = hand_on(place)
    cat0 = lambda *a: jnp.concatenate(a, axis=0)
    cat1 = lambda *a: jnp.concatenate(a, axis=1)

    local = dot_nt(after(cat0(probe_a, a_down), place), inputs)
    across, ahead_y, behind = go_y(local, 2), go_y(local, 1), go_y(local, -1)

    factors = (b_gate, b_up, probe_bg, probe_bu)
    rows = tokens // (NZ * NX)
    cut4 = lambda v: v.reshape(NZ, NX, rows, v.shape[1])
    c1, c2, gu, pq = early(gate_pre, up_pre, upstream, factors)
    early_out = (cut4(c1), cut4(c2), cut4(pq))
    tot = (after(local, c1) + across) + (ahead_y + behind)
    weights = (gate_weight, up_weight, a_down, probe_a)
    blocks = [(k, 2) for k in range(NZ)] + [(4, j) for j in range(NX)]
    blocks += [("p", n, x) for n in range(2) for x in range(NX)]
    a2, b4 = ahead(
        blocks, ((0, 8, 0), (8, 4, ca)), place, early_out, tot, factors, *weights, ca, "send_first", rank_blocks=12
    )
    xs = send(go_x, *a2)
    zs = send(go_z, *b4)

    blocks = [(k, j) for k in (3, 5) for j in range(NX)]
    b3, b5 = ahead(
        blocks, ((0, 4, ca), (4, 4, ca)), place, early_out, after(tot, *a2), factors, *weights, ca, "send_second"
    )
    zr, zl = together(after(zs[0], *b3), zs[1])
    zo = together(cat1(b3[0] + zr, b3[1]), cat1(b5[0], b5[1] + zl))
    zs = send(go_z, *zo)

    blocks = [(k, j) for j in (1, 3) for k in range(NZ)]
    a1, a3 = ahead(
        blocks, ((0, 8, 0), (8, 8, 0)), place, early_out, after(tot, *zo), factors, *weights, ca, "send_third"
    )
    kept = a1[0].shape[0]
    xr, xl = together(after(xs[0], *a1), xs[1])
    own, beside, behind = a2[0][kept:], xl[kept:], xr[kept:]
    xo = together(
        cat0(cat1(a1[0] + xr[:kept], a1[1]), cat1(behind, behind)), cat1(a3[0], a3[1] + xl[:kept])
    )
    xs = send(go_x, *xo)

    *one, hg1, hu1 = body(
        (2, 6, 1, 7), place, c1, c2, gu, pq, up_pre, after(tot, *xo), factors, "body_first"
    )
    cb = gate_weight.shape[0] - ca
    b2, b6, b1, b7 = terms([one], (([(0, n) for n in range(4)], ca, cb, 4),), *weights, "terms_first")
    zp, zm = together(after(zs[0], b2), zs[1])
    zo = together(b2 + zp, b6 + zm)
    zs = send(go_z, *zo)

    *two, hg2, hu2 = body(
        (0, 3, 4, 5), place, c1, c2, gu, pq, up_pre, after(tot, *zo), factors, "body_second", LONG
    )
    at = [(1, 0), (0, 2), (0, 0), (1, 1), (1, 2), (1, 3), (0, 1), (0, 3)]
    a0, b0 = terms(
        [one, two],
        (([(source, (n, 0)) for source, n in at], 0, ca, 1), ([(1, 0)], ca, cb, 1)),
        *weights, "terms_second",
    )
    xp, xm = together(after(xs[0], a0), xs[1])
    asum = a0 + xp[:kept] + xm
    part = (own + xp[kept:, :own.shape[1]]) + (beside + behind)

    cut = lambda v, k: v[k * rows:(k + 1) * rows]
    t = {k: cut(asum, k) for k in range(NZ)}
    upper = rows // 2
    zp, zm = together(after(zs[0], asum), zs[1])
    zo = together(cat0(b1 + zp, t[4][:upper]), cat0(b7 + zm, t[4][upper:]))
    zs = send(go_z, *zo)
    hvp_b = cat0(hg1 + hg2, hu1 + hu2)
    hvp_b = hvp_b + swap_core(after(hvp_b, *zo))
    part = part + pair_z(after(part, hvp_b), 1)
    part_z = pair_z(part, 2)

    kept = b0.shape[0]
    zp, zm = together(after(zs[0], part), zs[1])
    ao = together(
        cat0(t[3][:upper] + zp[kept:], t[3][upper:]), cat0(t[5][:upper], t[5][upper:] + zm[kept:])
    )
    az = send(go_z, *ao)
    bsum = b0 + zp[:kept] + zm[:kept]
    quarter = {j: cut(bsum, j) for j in range(NX)}
    bo = together(quarter[2][:upper], quarter[2][upper:])
    bx = send(go_x, *bo)
    part = part + after(part_z, *ao, *bo)
    part_z = pair_z(part, 4)

    ap, am = together(*az)
    ao = together(t[2] + ap, t[6] + am)
    az = send(go_z, *ao)
    xr, xl = together(after(bx[0], *ao), bx[1])
    bo = together(
        cat0(quarter[1][:upper] + xr, quarter[1][upper:]), cat0(quarter[3][:upper], quarter[3][upper:] + xl)
    )
    bx = send(go_x, *bo)
    part = part + after(part_z, *bo)
    p1 = go_y(part, -1)
    ap, am = together(after(az[0], part), az[1])
    ao = together(t[1] + ap, t[7] + am)
    az = send(go_z, *ao)
    xp, xm = together(after(bx[0], *ao), bx[1])
    p2, p3 = go_y(after(part, xp), 2), go_y(after(part, xp), 1)
    ap, am = together(*az)
    right = quarter[0] + xp + xm
    left = t[0] + ap + am
    input_tangent = cat1(left, right)

    hvp_a = width_sum(place, (part, p1, p2, p3), inputs)
    hvp_a = hvp_a + swap_core(hvp_a)

    token_count = tokens * lax.axis_size("dp")
    scale_b = math.sqrt(token_count)
    scale_a = math.sqrt(token_count * FF)
    next_a = 2.0 * probe_a.astype(F32) - hvp_a / scale_a
    next_bg = 2.0 * probe_bg.astype(F32) - hvp_b[:16] / scale_b
    next_bu = 2.0 * probe_bu.astype(F32) - hvp_b[16:] / scale_b
    return (input_tangent, next_a, next_bg, next_bu)


def solution(mesh):
    return jax.shard_map(
        shards,
        mesh=mesh,
        in_specs=(
            P("dp", "inp"),
            P("dp", "out"),
            P("dp", "out"),
            P("dp", "out"),
            P("inp", "out"),
            P("inp", "out"),
            P(None, "inp"),
            P(None, "out"),
            P(None, "out"),
            P(None, "inp"),
            P(None, "out"),
            P(None, "out"),
        ),
        out_specs=(P(("dp", "out"), "inp"), P(None, "inp"), P(None, "out"), P(None, "out")),
        check_vma=False,
    )
```

```python
import functools
import math

import jax
import jax.numpy as jnp
from jax import lax
from jax.experimental import pallas as pl
from jax.experimental.pallas import tpu as pltpu
from jax.sharding import PartitionSpec as P

FF = 28672
NX, NZ = 4, 8
F32, BF16 = jnp.float32, jnp.bfloat16
LANES = 128


def dot_nt(left, right):
    return lax.dot_general(left, right, (((1,), (1,)), ((), ())), preferred_element_type=F32)


def dot_nn(left, right):
    return lax.dot_general(left, right, (((1,), (0,)), ((), ())), preferred_element_type=F32)


def dot_tn(left, right):
    return lax.dot_general(left, right, (((0,), (0,)), ((), ())), preferred_element_type=F32)


def split2(value):
    high = value.astype(BF16)
    return high, (value - high.astype(F32)).astype(BF16)


def split3(value):
    high = value.astype(BF16)
    rest = value - high.astype(F32)
    mid = rest.astype(BF16)
    return high, mid, (rest - mid.astype(F32)).astype(BF16)


def params(mib=26):
    return pltpu.CompilerParams(vmem_limit_bytes=mib * 1024 * 1024)


VMEM = pl.BlockSpec(memory_space=pltpu.VMEM)
SMEM = pl.BlockSpec(memory_space=pltpu.SMEM)
COST = pl.CostEstimate(flops=1000, bytes_accessed=1000, transcendentals=0)
LONG = pl.CostEstimate(flops=24_000_000_000, bytes_accessed=90_000_000, transcendentals=0)


def early_tables(rg, ru, bg_ref, bu_ref, pg_ref, pu_ref):
    for ref, first, second in ((rg, pg_ref, bg_ref), (ru, pu_ref, bu_ref)):
        ref[...] = jnp.zeros_like(ref)
        ref[0:16] = first[...]
        ref[16:32] = second[...]


def tangent_tables(bst, rp, bg_ref, bu_ref, pg_ref, pu_ref):
    width = bg_ref.shape[1]
    for n in range(0, 96, 32):
        bst[n:n + 16, :width] = bg_ref[...]
        bst[n:n + 16, width:] = bu_ref[...]
        bst[n + 16:n + 32, :width] = pg_ref[...]
        bst[n + 16:n + 32, width:] = pu_ref[...]
    rp[...] = jnp.zeros_like(rp)
    rp[0, 0:16] = bg_ref[...]
    rp[1, 0:16] = bu_ref[...]


def rank_table(aa, a_ref, pa_ref):
    aa[...] = jnp.zeros_like(aa)
    for n in (0, 32):
        aa[n:n + 16] = a_ref[...]
        aa[n + 16:n + 32] = pa_ref[...]


def elementwise(g, u, dy):
    g, u, dy = g.astype(F32), u.astype(F32), dy.astype(F32)
    sig = 1.0 / (1.0 + jnp.exp(-g))
    rest = 1.0 - sig
    s = g * sig
    c1 = dy * (sig + s * rest)
    c2 = dy * u * (rest * (2.0 * sig + s - 2.0 * s * sig))
    return c1, c2, c1 * u, dy * s


def rank_terms(gg, gu, rg, ru):
    gg_hi, gg_lo = split2(gg)
    gu_hi, gu_lo = split2(gu)
    return (dot_nt(gg_hi, rg) + dot_nt(gg_lo, rg)) + (dot_nt(gu_hi, ru) + dot_nt(gu_lo, ru))


def tangent_math(both, c1, c2, pq, rpg, rpu):
    width = c1.shape[1]
    tang_g, tang_u = both[:, :width], both[:, width:]
    tgg = (tang_u * c1 + c2 * tang_g).astype(BF16)
    tgu = (c1 * tang_g).astype(BF16)
    pq = pq + (dot_nt(tgg, rpg) + dot_nt(tgu, rpu))
    high = pq.astype(BF16).astype(F32)
    return tgg, tgu, pq, (high + pltpu.roll(pq - high, 32, 1)).astype(BF16)


def body_kernel(place, c1_ref, c2_ref, gu_ref, pq_ref, u_ref, tot_ref, bg_ref, bu_ref, pg_ref, pu_ref,
                tgg_ref, tgu_ref, pqs_ref, hg_ref, hu_ref, bst, rp):
    first = pl.program_id(0) == 0

    @pl.when(first)
    def _():
        tangent_tables(bst, rp, bg_ref, bu_ref, pg_ref, pu_ref)

    c1 = c1_ref[...]
    tot = tot_ref[...]
    both = dot_tn(jnp.concatenate(split3(tot), axis=0), bst[...])
    tgg, tgu, _, full = tangent_math(both, c1, c2_ref[...], pq_ref[...], rp[0], rp[1])
    rows = tgg.shape[0] // NX
    for xx in range(NX):
        j = lax.rem(xx - place[1] + NX, NX)
        part = slice(xx * rows, (xx + 1) * rows)
        tgg_ref[0, j] = tgg[part]
        tgu_ref[0, j] = tgu[part]
        pqs_ref[0, j] = full[part]

    t_hi, t_lo = split2(tot)
    xv = jnp.concatenate([t_hi[:16], t_lo[:16]], axis=0)
    xa = jnp.concatenate([t_hi[16:], t_lo[16:]], axis=0)

    def both_terms(grad, tan):
        hi, lo = split2(grad)
        sums = dot_nn(xv, hi) + dot_nn(xa, tan)
        return sums[:16] + sums[16:] + dot_nn(xv[:16], lo)

    hg = both_terms(c1 * u_ref[...].astype(F32), tgg)
    hu = both_terms(gu_ref[...], tgu)

    @pl.when(first)
    def _():
        hg_ref[...] = hg
        hu_ref[...] = hu

    @pl.when(jnp.logical_not(first))
    def _():
        hg_ref[...] += hg
        hu_ref[...] += hu


def body(order, place, c1, c2, gu, pq, u, tot, factors, name, cost=COST):
    tokens, width = u.shape
    block = tokens // NZ
    rows = block // NX

    def nat(i, s):
        k = order[-1]
        for n, value in enumerate(order[:-1]):
            k = jnp.where(i == n, value, k)
        return lax.rem(k + s[0], NZ)

    row = pl.BlockSpec((block, width), lambda i, s: (nat(i, s), 0))
    rel = lambda n: pl.BlockSpec((1, NX, rows, n), lambda i, s: (i, 0, 0, 0))
    rank = pl.BlockSpec((16, width), lambda i, s: (0, 0))
    return pl.pallas_call(
        body_kernel,
        grid_spec=pltpu.PrefetchScalarGridSpec(
            num_scalar_prefetch=1,
            grid=(len(order),),
            in_specs=[
                row, row, row,
                pl.BlockSpec((block, LANES), lambda i, s: (nat(i, s), 0)),
                row,
                pl.BlockSpec((32, block), lambda i, s: (0, nat(i, s))),
                rank, rank, rank, rank,
            ],
            out_specs=[rel(width), rel(width), rel(LANES), rank, rank],
            scratch_shapes=[pltpu.VMEM((96, 2 * width), BF16), pltpu.VMEM((2, LANES, width), BF16)],
        ),
        out_shape=[
            jax.ShapeDtypeStruct((len(order), NX, rows, width), BF16),
            jax.ShapeDtypeStruct((len(order), NX, rows, width), BF16),
            jax.ShapeDtypeStruct((len(order), NX, rows, LANES), BF16),
            jax.ShapeDtypeStruct((16, width), F32),
            jax.ShapeDtypeStruct((16, width), F32),
        ],
        compiler_params=params(20),
        cost_estimate=cost,
        name=name,
    )(place, c1, c2, gu, pq, u, tot, *factors)


def terms_kernel(sources, jobs, gw_ref, uw_ref, a_ref, pa_ref, *rest):
    ins, outs, aa = rest[:3 * sources], rest[3 * sources:-1], rest[-1]
    rank_table(aa, a_ref, pa_ref)
    step = 256
    done = 0
    for blocks, low, columns, parts in jobs:
        def left(which):
            got = [ins[3 * source + which][index].reshape(-1, ins[3 * source + which].shape[-1])
                   for source, index in blocks]
            return got[0] if len(got) == 1 else jnp.concatenate(got, axis=0)

        lg, lu, lp = left(0), left(1), left(2)
        n = lg.shape[0] // parts
        for c in range(0, columns, step):
            cols = slice(low + c, low + c + step)
            value = (dot_nt(lg, gw_ref[cols]) + dot_nt(lu, uw_ref[cols])) + dot_nn(lp, aa[:, cols])
            for m in range(parts):
                outs[done + m][:, c:c + step] = value[m * n:(m + 1) * n]
        done += parts


def terms(bodies, jobs, gw, uw, a_down, probe_a, name):
    nx, rows = bodies[0][0].shape[1:3]
    shapes = []
    for blocks, _, columns, parts in jobs:
        count = sum(bodies[source][0][index].size for source, index in blocks) // bodies[0][0].shape[-1]
        shapes += [jax.ShapeDtypeStruct((count // parts, columns), F32)] * parts
    flat = [v for three in bodies for v in three]
    return pl.pallas_call(
        functools.partial(terms_kernel, len(bodies), jobs),
        in_specs=[VMEM] * (4 + len(flat)),
        out_specs=[VMEM] * len(shapes),
        out_shape=shapes,
        scratch_shapes=[pltpu.VMEM((LANES, gw.shape[0]), BF16)],
        compiler_params=params(18),
        cost_estimate=COST,
        name=name,
    )(gw, uw, a_down, probe_a, *flat)


def early_kernel(g_ref, u_ref, dy_ref, bg_ref, bu_ref, pg_ref, pu_ref, c1_ref, c2_ref, gu_ref, pq_ref, rg, ru):
    early_tables(rg, ru, bg_ref, bu_ref, pg_ref, pu_ref)
    block = g_ref.shape[0] // 8
    for n in range(8):
        rows = slice(n * block, (n + 1) * block)
        c1, c2, gg, gu = elementwise(g_ref[rows], u_ref[rows], dy_ref[rows])
        c1_ref[rows] = c1
        c2_ref[rows] = c2
        gu_ref[rows] = gu
        pq_ref[rows] = rank_terms(gg, gu, rg[...], ru[...])


def early(g, u, dy, factors):
    tokens, width = g.shape
    wide = jax.ShapeDtypeStruct((tokens, width), F32)
    return pl.pallas_call(
        early_kernel,
        in_specs=[VMEM] * 7,
        out_specs=[VMEM] * 4,
        out_shape=[wide, wide, wide, jax.ShapeDtypeStruct((tokens, LANES), F32)],
        scratch_shapes=[pltpu.VMEM((LANES, width), BF16), pltpu.VMEM((LANES, width), BF16)],
        compiler_params=params(22),
        cost_estimate=COST,
        name="early",
    )(g, u, dy, *factors)


def block_at(place, block):
    if len(block) == 3:
        return 2 * place[2] + block[1], block[2]
    return lax.rem(place[0] + block[0], NZ), lax.rem(place[1] + block[1], NX)


def ahead_kernel(blocks, groups, rank_blocks, place, c1_ref, c2_ref, pq_ref, tot_ref, bg_ref, bu_ref,
                 pg_ref, pu_ref, gw_ref, uw_ref, a_ref, pa_ref, *rest):
    outs, (tot_rows, bst, rp, aa) = rest[:-4], rest[-4:]
    rows = tot_rows.shape[1]
    tot_rows[...] = tot_ref[...].T.reshape(tot_rows.shape)
    tangent_tables(bst, rp, bg_ref, bu_ref, pg_ref, pu_ref)
    rank_table(aa, a_ref, pa_ref)
    at = [block_at(place, block) for block in blocks]
    gather = lambda ref: jnp.concatenate([ref[z, x] for z, x in at], axis=0)
    tot = jnp.concatenate([tot_rows[z * NX + x] for z, x in at], axis=0)
    both = dot_nn(jnp.concatenate(split3(tot), axis=1), bst[...])
    tgg, tgu, pq, full = tangent_math(both, gather(c1_ref), gather(c2_ref), gather(pq_ref), rp[0], rp[1])
    if rank_blocks is not None:
        low = rank_blocks * rows
        for n in range(0, pq.shape[0] - low, LANES):
            turned = pq[low + n:low + n + LANES].T
            for ref in outs[:2]:
                ref[-8:, n:n + LANES] = turned[0:8]
                ref[-8:, 256 + n:256 + n + LANES] = turned[8:16]
    step = 256
    lows = sorted({low for _, _, low in groups})
    for low in lows:
        mine = [(g, start, count) for g, (start, count, at_low) in enumerate(groups) if at_low == low]
        base, total = mine[0][1], sum(count for _, _, count in mine)
        part = slice(base * rows, (base + total) * rows)
        half = outs[2 * mine[0][0]].shape[1]
        for c in range(0, 2 * half, step):
            cols = slice(low + c, low + c + step)
            value = (
                dot_nt(tgg[part], gw_ref[cols]) + dot_nt(tgu[part], uw_ref[cols])
            ) + dot_nn(full[part], aa[:, cols])
            for g, start, count in mine:
                first = (start - base) * rows
                outs[2 * g + c // half][:count * rows, c % half:c % half + step] = value[first:first + count * rows]


def ahead(blocks, groups, place, early_out, tot, factors, gw, uw, a, pa, ca, name, rank_blocks=None):
    rows, width = early_out[0].shape[2:]
    model = gw.shape[0]
    shapes = []
    for g, (_, count, low) in enumerate(groups):
        columns = model - ca if low else ca
        more = 8 if g == 0 and rank_blocks is not None else 0
        shapes += [jax.ShapeDtypeStruct((count * rows + more, columns // 2), F32)] * 2
    outs = pl.pallas_call(
        functools.partial(ahead_kernel, blocks, groups, rank_blocks),
        in_specs=[SMEM] + [VMEM] * 12,
        out_specs=[VMEM] * len(shapes),
        out_shape=shapes,
        scratch_shapes=[
            pltpu.VMEM((NZ * NX, rows, 32), F32),
            pltpu.VMEM((96, 2 * width), BF16),
            pltpu.VMEM((2, LANES, width), BF16),
            pltpu.VMEM((LANES, model), BF16),
        ],
        compiler_params=params(20),
        cost_estimate=COST,
        name=name,
    )(place, *early_out, tot, *factors, gw, uw, a, pa)
    return [tuple(outs[2 * g:2 * g + 2]) for g in range(len(groups))]


def width_kernel(place, p0_ref, p1_ref, p2_ref, p3_ref, x_ref, out_ref):
    quarter = p0_ref.shape[1] // 2
    total = None
    for n, ref in enumerate((p0_ref, p1_ref, p2_ref, p3_ref)):
        start = pl.multiple_of(lax.rem(place[2] + n, 4) * quarter, quarter)
        p = jnp.concatenate([ref[:, :quarter], ref[:, quarter:]], axis=0)
        part = dot_nn(jnp.concatenate(split3(p), axis=0), x_ref[pl.ds(start, quarter), :])
        part = part[:16] + (part[16:32] + part[32:])
        total = part if total is None else total + part
    out_ref[...] = total


def width_sum(place, quarters, inputs):
    return pl.pallas_call(
        width_kernel,
        in_specs=[SMEM] + [VMEM] * 5,
        out_specs=VMEM,
        out_shape=jax.ShapeDtypeStruct((16, inputs.shape[1]), F32),
        compiler_params=params(12),
        cost_estimate=COST,
        name="width_sum",
    )(place, *quarters, inputs)


def place_kernel(place_ref, out_ref):
    for n in range(3):
        out_ref[n] = place_ref[n]


def hand_on(place):
    return pl.pallas_call(
        place_kernel,
        in_specs=[SMEM],
        out_specs=SMEM,
        out_shape=jax.ShapeDtypeStruct((3,), jnp.int32),
        compiler_params=params(2),
        cost_estimate=LONG,
        name="hand_on",
    )(place)


def out_perm(dz, dx):
    return [(z * NX + x, ((z + dz) % NZ) * NX + (x + dx) % NX) for z in range(NZ) for x in range(NX)]


def go_x(value, d):
    return lax.ppermute(value, "out", out_perm(0, d))


def go_z(value, d):
    return lax.ppermute(value, "out", out_perm(d, 0))


def go_y(value, d):
    return lax.ppermute(value, "inp", [(i, (i + d) % 4) for i in range(4)])


def pair_x(value, mask):
    return lax.ppermute(value, "out", [(z * NX + x, z * NX + (x ^ mask)) for z in range(NZ) for x in range(NX)])


def pair_z(value, mask):
    return lax.ppermute(value, "out", [(z * NX + x, (z ^ mask) * NX + x) for z in range(NZ) for x in range(NX)])


def swap_core(value):
    return lax.ppermute(value, "dp", [(0, 1), (1, 0)])


def send(go, ahead_value, back_value):
    return go(ahead_value, 1), go(back_value, -1)


def together(*values):
    return lax.optimization_barrier(values)


def after(value, *others):
    return lax.optimization_barrier((value,) + others)[0]


def shards(inputs, gate_pre, up_pre, upstream, gate_weight, up_weight,
           a_down, b_gate, b_up, probe_a, probe_bg, probe_bu):
    tokens = inputs.shape[0]
    ca = gate_weight.shape[0] // 2
    at = lax.axis_index("out")
    place = jnp.stack([at >> 2, at & 3, lax.axis_index("inp")]).astype(jnp.int32)
    place = hand_on(place)
    cat0 = lambda *a: jnp.concatenate(a, axis=0)
    cat1 = lambda *a: jnp.concatenate(a, axis=1)

    local = dot_nt(after(cat0(probe_a, a_down), place), inputs)
    across, ahead_y, behind = go_y(local, 2), go_y(local, 1), go_y(local, -1)

    factors = (b_gate, b_up, probe_bg, probe_bu)
    rows = tokens // (NZ * NX)
    cut4 = lambda v: v.reshape(NZ, NX, rows, v.shape[1])
    c1, c2, gu, pq = early(gate_pre, up_pre, upstream, factors)
    early_out = (cut4(c1), cut4(c2), cut4(pq))
    tot = (after(local, c1) + across) + (ahead_y + behind)
    weights = (gate_weight, up_weight, a_down, probe_a)
    blocks = [(k, 2) for k in range(NZ)] + [(4, j) for j in range(NX)]
    blocks += [("p", n, x) for n in range(2) for x in range(NX)]
    a2, b4 = ahead(
        blocks, ((0, 8, 0), (8, 4, ca)), place, early_out, tot, factors, *weights, ca, "send_first", rank_blocks=12
    )
    xs = send(go_x, *a2)
    zs = send(go_z, *b4)

    blocks = [(k, j) for j in (1, 3) for k in range(NZ)]
    a1, a3 = ahead(
        blocks, ((0, 8, 0), (8, 8, 0)), place, early_out, after(tot, *a2), factors, *weights, ca, "send_second"
    )
    blocks = [(k, j) for k in (3, 5) for j in range(NX)]
    b3, b5 = ahead(
        blocks, ((0, 4, ca), (4, 4, ca)), place, early_out, after(tot, *a1), factors, *weights, ca, "send_third"
    )
    zr, zl = together(after(zs[0], *b3), zs[1])
    zo = together(cat1(b3[0] + zr, b3[1]), cat1(b5[0], b5[1] + zl))
    zs = send(go_z, *zo)

    kept = a1[0].shape[0]
    xr, xl = together(after(xs[0], *zo), xs[1])
    own, beside, behind = together(a2[0][kept:], xl[kept:], xr[kept:])
    xo = together(
        cat0(cat1(a1[0] + xr[:kept], a1[1]), cat1(behind, behind)), cat1(a3[0], a3[1] + xl[:kept])
    )
    xs = send(go_x, *xo)

    *one, hg1, hu1 = body(
        (2, 6), place, c1, c2, gu, pq, up_pre, after(tot, *xo), factors, "body_first"
    )
    cb = gate_weight.shape[0] - ca
    b2, b6 = terms([one], (([(0, 0), (0, 1)], ca, cb, 2),), *weights, "terms_first")
    zp, zm = together(after(zs[0], b2), zs[1])
    zo = together(b2 + zp, b6 + zm)
    zs = send(go_z, *zo)

    *two, hg2, hu2 = body(
        (1, 7, 0, 3, 4, 5), place, c1, c2, gu, pq, up_pre, after(tot, *zo), factors, "body_second", LONG
    )
    at = [(1, 2), (1, 0), (0, 0), (1, 3), (1, 4), (1, 5), (0, 1), (1, 1)]
    a0, b1, b7, b0 = terms(
        [one, two],
        (([(source, (n, 0)) for source, n in at], 0, ca, 1), ([(1, 0), (1, 1), (1, 2)], ca, cb, 3)),
        *weights, "terms_second",
    )
    xp, xm = together(after(xs[0], a0), xs[1])
    asum = a0 + xp[:kept] + xm
    part = (own + xp[kept:, :own.shape[1]]) + (beside + behind)

    cut = lambda v, k: v[k * rows:(k + 1) * rows]
    t = {k: cut(asum, k) for k in range(NZ)}
    upper = rows // 2
    zp, zm = together(after(zs[0], asum), zs[1])
    zo = together(cat0(b1 + zp, t[4][:upper]), cat0(b7 + zm, t[4][upper:]))
    zs = send(go_z, *zo)
    hvp_b = cat0(hg1 + hg2, hu1 + hu2)
    hvp_b = hvp_b + swap_core(after(hvp_b, *zo))
    part_z = pair_z(after(part, hvp_b), 4)
    zp, zm = together(*zs)
    part = part + after(part_z, zp)

    kept = b0.shape[0]
    double = cat1(part, part)
    ao = together(
        cat0(t[3][:upper] + zp[kept:], t[3][upper:], t[1], double),
        cat0(t[5][:upper], t[5][upper:] + zm[kept:], t[7], double),
    )
    az = send(go_z, *ao)
    bsum = b0 + zp[:kept] + zm[:kept]
    quarter = {j: cut(bsum, j) for j in range(NX)}
    bo = together(quarter[1], quarter[3], part)
    bx = send(go_x, bo[0], bo[1])
    part_z = pair_z(bo[2], 2)

    ap, am = together(*az)
    ao = together(t[2] + ap[:rows], t[6] + am[:rows])
    az = go_z(ao[0], 2), go_z(ao[1], -2)
    far = go_x(after(quarter[2], *ao), 2)
    width = part.shape[1]
    part = (part + after(part_z, *ao, *bx)) + (ap[2 * rows:, :width] + am[2 * rows:, :width])
    p1, p2, p3 = go_y(part, -1), go_y(part, 2), go_y(part, 1)
    right = (quarter[0] + far) + (bx[0] + bx[1])
    left = (t[0] + ap[rows:2 * rows] + am[rows:2 * rows]) + (az[0] + az[1])
    input_tangent = cat1(left, right)

    hvp_a = width_sum(place, (part, p1, p2, p3), inputs)
    hvp_a = hvp_a + swap_core(hvp_a)

    token_count = tokens * lax.axis_size("dp")
    scale_b = math.sqrt(token_count)
    scale_a = math.sqrt(token_count * FF)
    next_a = 2.0 * probe_a.astype(F32) - hvp_a / scale_a
    next_bg = 2.0 * probe_bg.astype(F32) - hvp_b[:16] / scale_b
    next_bu = 2.0 * probe_bu.astype(F32) - hvp_b[16:] / scale_b
    return (input_tangent, next_a, next_bg, next_bu)


def solution(mesh):
    return jax.shard_map(
        shards,
        mesh=mesh,
        in_specs=(
            P("dp", "inp"),
            P("dp", "out"),
            P("dp", "out"),
            P("dp", "out"),
            P("inp", "out"),
            P("inp", "out"),
            P(None, "inp"),
            P(None, "out"),
            P(None, "out"),
            P(None, "inp"),
            P(None, "out"),
            P(None, "out"),
        ),
        out_specs=(P(("dp", "out"), "inp"), P(None, "inp"), P(None, "out"), P(None, "out")),
        check_vma=False,
    )
```

```python
import functools
import math

import jax
import jax.numpy as jnp
from jax import lax
from jax.experimental import pallas as pl
from jax.experimental.pallas import tpu as pltpu
from jax.sharding import PartitionSpec as P

FF = 28672
NX, NZ = 4, 8
F32, BF16 = jnp.float32, jnp.bfloat16
LANES = 128


def dot_nt(left, right):
    return lax.dot_general(left, right, (((1,), (1,)), ((), ())), preferred_element_type=F32)


def dot_nn(left, right):
    return lax.dot_general(left, right, (((1,), (0,)), ((), ())), preferred_element_type=F32)


def dot_tn(left, right):
    return lax.dot_general(left, right, (((0,), (0,)), ((), ())), preferred_element_type=F32)


def split2(value):
    high = value.astype(BF16)
    return high, (value - high.astype(F32)).astype(BF16)


def split3(value):
    high = value.astype(BF16)
    rest = value - high.astype(F32)
    mid = rest.astype(BF16)
    return high, mid, (rest - mid.astype(F32)).astype(BF16)


def params(mib=26):
    return pltpu.CompilerParams(vmem_limit_bytes=mib * 1024 * 1024)


VMEM = pl.BlockSpec(memory_space=pltpu.VMEM)
SMEM = pl.BlockSpec(memory_space=pltpu.SMEM)
COST = pl.CostEstimate(flops=1000, bytes_accessed=1000, transcendentals=0)
LONG = pl.CostEstimate(flops=24_000_000_000, bytes_accessed=90_000_000, transcendentals=0)


def early_tables(rg, ru, bg_ref, bu_ref, pg_ref, pu_ref):
    for ref, first, second in ((rg, pg_ref, bg_ref), (ru, pu_ref, bu_ref)):
        ref[...] = jnp.zeros_like(ref)
        ref[0:16] = first[...]
        ref[16:32] = second[...]


def tangent_tables(bst, rp, bg_ref, bu_ref, pg_ref, pu_ref):
    width = bg_ref.shape[1]
    for n in range(0, 96, 32):
        bst[n:n + 16, :width] = bg_ref[...]
        bst[n:n + 16, width:] = bu_ref[...]
        bst[n + 16:n + 32, :width] = pg_ref[...]
        bst[n + 16:n + 32, width:] = pu_ref[...]
    rp[...] = jnp.zeros_like(rp)
    rp[0, 0:16] = bg_ref[...]
    rp[1, 0:16] = bu_ref[...]


def rank_table(aa, a_ref, pa_ref):
    aa[...] = jnp.zeros_like(aa)
    for n in (0, 32):
        aa[n:n + 16] = a_ref[...]
        aa[n + 16:n + 32] = pa_ref[...]


def elementwise(g, u, dy):
    g, u, dy = g.astype(F32), u.astype(F32), dy.astype(F32)
    sig = 1.0 / (1.0 + jnp.exp(-g))
    s = g * sig
    c1 = dy * (sig + (s - s * sig))
    gu = dy * s
    c2 = u * ((1.0 - sig) * (c1 + c1 - gu))
    return c1, c2, c1 * u, gu


def rank_terms(gg, gu, rg, ru):
    gg_hi, gg_lo = split2(gg)
    gu_hi, gu_lo = split2(gu)
    return (dot_nt(gg_hi, rg) + dot_nt(gg_lo, rg)) + (dot_nt(gu_hi, ru) + dot_nt(gu_lo, ru))


def tangent_math(both, c1, c2, pq, rpg, rpu):
    width = c1.shape[1]
    tang_g, tang_u = both[:, :width], both[:, width:]
    tgg = (tang_u * c1 + c2 * tang_g).astype(BF16)
    tgu = (c1 * tang_g).astype(BF16)
    pq = pq + (dot_nt(tgg, rpg) + dot_nt(tgu, rpu))
    high = pq.astype(BF16).astype(F32)
    return tgg, tgu, pq, (high + pltpu.roll(pq - high, 32, 1)).astype(BF16)


def body_kernel(place, c1_ref, c2_ref, gu_ref, pq_ref, u_ref, tot_ref, bg_ref, bu_ref, pg_ref, pu_ref,
                tgg_ref, tgu_ref, pqs_ref, hg_ref, hu_ref, bst, rp):
    first = pl.program_id(0) == 0

    @pl.when(first)
    def _():
        tangent_tables(bst, rp, bg_ref, bu_ref, pg_ref, pu_ref)

    c1 = c1_ref[...]
    tot = tot_ref[...]
    both = dot_tn(jnp.concatenate(split3(tot), axis=0), bst[...])
    tgg, tgu, _, full = tangent_math(both, c1, c2_ref[...], pq_ref[...], rp[0], rp[1])
    rows = tgg.shape[0] // NX
    for xx in range(NX):
        j = lax.rem(xx - place[1] + NX, NX)
        part = slice(xx * rows, (xx + 1) * rows)
        tgg_ref[0, j] = tgg[part]
        tgu_ref[0, j] = tgu[part]
        pqs_ref[0, j] = full[part]

    t_hi, t_lo = split2(tot)
    xv = jnp.concatenate([t_hi[:16], t_lo[:16]], axis=0)
    xa = jnp.concatenate([t_hi[16:], t_lo[16:]], axis=0)

    def both_terms(grad, tan):
        hi, lo = split2(grad)
        sums = dot_nn(xv, hi) + dot_nn(xa, tan)
        return sums[:16] + sums[16:] + dot_nn(xv[:16], lo)

    hg = both_terms(c1 * u_ref[...].astype(F32), tgg)
    hu = both_terms(gu_ref[...], tgu)

    @pl.when(first)
    def _():
        hg_ref[...] = hg
        hu_ref[...] = hu

    @pl.when(jnp.logical_not(first))
    def _():
        hg_ref[...] += hg
        hu_ref[...] += hu


def body(order, place, c1, c2, gu, pq, u, tot, factors, name, cost=COST):
    tokens, width = u.shape
    block = tokens // NZ
    rows = block // NX

    def nat(i, s):
        k = order[-1]
        for n, value in enumerate(order[:-1]):
            k = jnp.where(i == n, value, k)
        return lax.rem(k + s[0], NZ)

    row = pl.BlockSpec((block, width), lambda i, s: (nat(i, s), 0))
    rel = lambda n: pl.BlockSpec((1, NX, rows, n), lambda i, s: (i, 0, 0, 0))
    rank = pl.BlockSpec((16, width), lambda i, s: (0, 0))
    return pl.pallas_call(
        body_kernel,
        grid_spec=pltpu.PrefetchScalarGridSpec(
            num_scalar_prefetch=1,
            grid=(len(order),),
            in_specs=[
                row, row, row,
                pl.BlockSpec((block, LANES), lambda i, s: (nat(i, s), 0)),
                row,
                pl.BlockSpec((32, block), lambda i, s: (0, nat(i, s))),
                rank, rank, rank, rank,
            ],
            out_specs=[rel(width), rel(width), rel(LANES), rank, rank],
            scratch_shapes=[pltpu.VMEM((96, 2 * width), BF16), pltpu.VMEM((2, LANES, width), BF16)],
        ),
        out_shape=[
            jax.ShapeDtypeStruct((len(order), NX, rows, width), BF16),
            jax.ShapeDtypeStruct((len(order), NX, rows, width), BF16),
            jax.ShapeDtypeStruct((len(order), NX, rows, LANES), BF16),
            jax.ShapeDtypeStruct((16, width), F32),
            jax.ShapeDtypeStruct((16, width), F32),
        ],
        compiler_params=params(20),
        cost_estimate=cost,
        name=name,
    )(place, c1, c2, gu, pq, u, tot, *factors)


def terms_kernel(sources, jobs, gw_ref, uw_ref, a_ref, pa_ref, *rest):
    ins, outs, aa = rest[:3 * sources], rest[3 * sources:-1], rest[-1]
    rank_table(aa, a_ref, pa_ref)
    step = 256
    done = 0
    for blocks, low, columns, parts in jobs:
        def left(which):
            got = [ins[3 * source + which][index].reshape(-1, ins[3 * source + which].shape[-1])
                   for source, index in blocks]
            return got[0] if len(got) == 1 else jnp.concatenate(got, axis=0)

        lg, lu, lp = left(0), left(1), left(2)
        n = lg.shape[0] // parts
        for c in range(0, columns, step):
            cols = slice(low + c, low + c + step)
            value = (dot_nt(lg, gw_ref[cols]) + dot_nt(lu, uw_ref[cols])) + dot_nn(lp, aa[:, cols])
            for m in range(parts):
                outs[done + m][:, c:c + step] = value[m * n:(m + 1) * n]
        done += parts


def terms(bodies, jobs, gw, uw, a_down, probe_a, name):
    nx, rows = bodies[0][0].shape[1:3]
    shapes = []
    for blocks, _, columns, parts in jobs:
        count = sum(bodies[source][0][index].size for source, index in blocks) // bodies[0][0].shape[-1]
        shapes += [jax.ShapeDtypeStruct((count // parts, columns), F32)] * parts
    flat = [v for three in bodies for v in three]
    return pl.pallas_call(
        functools.partial(terms_kernel, len(bodies), jobs),
        in_specs=[VMEM] * (4 + len(flat)),
        out_specs=[VMEM] * len(shapes),
        out_shape=shapes,
        scratch_shapes=[pltpu.VMEM((LANES, gw.shape[0]), BF16)],
        compiler_params=params(18),
        cost_estimate=COST,
        name=name,
    )(gw, uw, a_down, probe_a, *flat)


def early_kernel(g_ref, u_ref, dy_ref, bg_ref, bu_ref, pg_ref, pu_ref, c1_ref, c2_ref, gu_ref, pq_ref, rg, ru):
    early_tables(rg, ru, bg_ref, bu_ref, pg_ref, pu_ref)
    block = g_ref.shape[0] // 8
    for n in range(8):
        rows = slice(n * block, (n + 1) * block)
        c1, c2, gg, gu = elementwise(g_ref[rows], u_ref[rows], dy_ref[rows])
        c1_ref[rows] = c1
        c2_ref[rows] = c2
        gu_ref[rows] = gu
        pq_ref[rows] = rank_terms(gg, gu, rg[...], ru[...])


def early(g, u, dy, factors):
    tokens, width = g.shape
    wide = jax.ShapeDtypeStruct((tokens, width), F32)
    return pl.pallas_call(
        early_kernel,
        in_specs=[VMEM] * 7,
        out_specs=[VMEM] * 4,
        out_shape=[wide, wide, wide, jax.ShapeDtypeStruct((tokens, LANES), F32)],
        scratch_shapes=[pltpu.VMEM((LANES, width), BF16), pltpu.VMEM((LANES, width), BF16)],
        compiler_params=params(22),
        cost_estimate=COST,
        name="early",
    )(g, u, dy, *factors)


def block_at(place, block):
    if len(block) == 3:
        return 2 * place[2] + block[1], block[2]
    return lax.rem(place[0] + block[0], NZ), lax.rem(place[1] + block[1], NX)


def ahead_kernel(blocks, groups, rank_blocks, place, c1_ref, c2_ref, pq_ref, tot_ref, bg_ref, bu_ref,
                 pg_ref, pu_ref, gw_ref, uw_ref, a_ref, pa_ref, *rest):
    outs, (tot_rows, bst, rp, aa) = rest[:-4], rest[-4:]
    rows = tot_rows.shape[1]
    tot_rows[...] = tot_ref[...].T.reshape(tot_rows.shape)
    tangent_tables(bst, rp, bg_ref, bu_ref, pg_ref, pu_ref)
    rank_table(aa, a_ref, pa_ref)
    at = [block_at(place, block) for block in blocks]
    gather = lambda ref: jnp.concatenate([ref[z, x] for z, x in at], axis=0)
    tot = jnp.concatenate([tot_rows[z * NX + x] for z, x in at], axis=0)
    both = dot_nn(jnp.concatenate(split3(tot), axis=1), bst[...])
    tgg, tgu, pq, full = tangent_math(both, gather(c1_ref), gather(c2_ref), gather(pq_ref), rp[0], rp[1])
    if rank_blocks is not None:
        low = rank_blocks * rows
        for n in range(0, pq.shape[0] - low, LANES):
            turned = pq[low + n:low + n + LANES].T
            for ref in outs[:2]:
                ref[-8:, n:n + LANES] = turned[0:8]
                ref[-8:, 256 + n:256 + n + LANES] = turned[8:16]
    step = 256
    lows = sorted({low for _, _, low in groups})
    for low in lows:
        mine = [(g, start, count) for g, (start, count, at_low) in enumerate(groups) if at_low == low]
        base, total = mine[0][1], sum(count for _, _, count in mine)
        part = slice(base * rows, (base + total) * rows)
        half = outs[2 * mine[0][0]].shape[1]
        for c in range(0, 2 * half, step):
            cols = slice(low + c, low + c + step)
            value = (
                dot_nt(tgg[part], gw_ref[cols]) + dot_nt(tgu[part], uw_ref[cols])
            ) + dot_nn(full[part], aa[:, cols])
            for g, start, count in mine:
                first = (start - base) * rows
                outs[2 * g + c // half][:count * rows, c % half:c % half + step] = value[first:first + count * rows]


def ahead(blocks, groups, place, early_out, tot, factors, gw, uw, a, pa, ca, name, rank_blocks=None):
    rows, width = early_out[0].shape[2:]
    model = gw.shape[0]
    shapes = []
    for g, (_, count, low) in enumerate(groups):
        columns = model - ca if low else ca
        more = 8 if g == 0 and rank_blocks is not None else 0
        shapes += [jax.ShapeDtypeStruct((count * rows + more, columns // 2), F32)] * 2
    outs = pl.pallas_call(
        functools.partial(ahead_kernel, blocks, groups, rank_blocks),
        in_specs=[SMEM] + [VMEM] * 12,
        out_specs=[VMEM] * len(shapes),
        out_shape=shapes,
        scratch_shapes=[
            pltpu.VMEM((NZ * NX, rows, 32), F32),
            pltpu.VMEM((96, 2 * width), BF16),
            pltpu.VMEM((2, LANES, width), BF16),
            pltpu.VMEM((LANES, model), BF16),
        ],
        compiler_params=params(20),
        cost_estimate=COST,
        name=name,
    )(place, *early_out, tot, *factors, gw, uw, a, pa)
    return [tuple(outs[2 * g:2 * g + 2]) for g in range(len(groups))]


def width_kernel(place, p0_ref, p1_ref, p2_ref, p3_ref, x_ref, out_ref):
    quarter = p0_ref.shape[1] // 2
    total = None
    for n, ref in enumerate((p0_ref, p1_ref, p2_ref, p3_ref)):
        start = pl.multiple_of(lax.rem(place[2] + n, 4) * quarter, quarter)
        p = jnp.concatenate([ref[:, :quarter], ref[:, quarter:]], axis=0)
        part = dot_nn(jnp.concatenate(split3(p), axis=0), x_ref[pl.ds(start, quarter), :])
        part = part[:16] + (part[16:32] + part[32:])
        total = part if total is None else total + part
    out_ref[...] = total


def width_sum(place, quarters, inputs):
    return pl.pallas_call(
        width_kernel,
        in_specs=[SMEM] + [VMEM] * 5,
        out_specs=VMEM,
        out_shape=jax.ShapeDtypeStruct((16, inputs.shape[1]), F32),
        compiler_params=params(12),
        cost_estimate=COST,
        name="width_sum",
    )(place, *quarters, inputs)


def place_kernel(place_ref, out_ref):
    for n in range(3):
        out_ref[n] = place_ref[n]


def hand_on(place):
    return pl.pallas_call(
        place_kernel,
        in_specs=[SMEM],
        out_specs=SMEM,
        out_shape=jax.ShapeDtypeStruct((3,), jnp.int32),
        compiler_params=params(2),
        cost_estimate=LONG,
        name="hand_on",
    )(place)


def out_perm(dz, dx):
    return [(z * NX + x, ((z + dz) % NZ) * NX + (x + dx) % NX) for z in range(NZ) for x in range(NX)]


def go_x(value, d):
    return lax.ppermute(value, "out", out_perm(0, d))


def go_z(value, d):
    return lax.ppermute(value, "out", out_perm(d, 0))


def go_y(value, d):
    return lax.ppermute(value, "inp", [(i, (i + d) % 4) for i in range(4)])


def pair_x(value, mask):
    return lax.ppermute(value, "out", [(z * NX + x, z * NX + (x ^ mask)) for z in range(NZ) for x in range(NX)])


def pair_z(value, mask):
    return lax.ppermute(value, "out", [(z * NX + x, (z ^ mask) * NX + x) for z in range(NZ) for x in range(NX)])


def swap_core(value):
    return lax.ppermute(value, "dp", [(0, 1), (1, 0)])


def send(go, ahead_value, back_value):
    return go(ahead_value, 1), go(back_value, -1)


def together(*values):
    return lax.optimization_barrier(values)


def after(value, *others):
    return lax.optimization_barrier((value,) + others)[0]


def shards(inputs, gate_pre, up_pre, upstream, gate_weight, up_weight,
           a_down, b_gate, b_up, probe_a, probe_bg, probe_bu):
    tokens = inputs.shape[0]
    ca = gate_weight.shape[0] // 2
    at = lax.axis_index("out")
    place = jnp.stack([at >> 2, at & 3, lax.axis_index("inp")]).astype(jnp.int32)
    place = hand_on(place)
    cat0 = lambda *a: jnp.concatenate(a, axis=0)
    cat1 = lambda *a: jnp.concatenate(a, axis=1)

    local = dot_nt(after(cat0(probe_a, a_down), place), inputs)
    across, ahead_y, behind = go_y(local, 2), go_y(local, 1), go_y(local, -1)

    factors = (b_gate, b_up, probe_bg, probe_bu)
    rows = tokens // (NZ * NX)
    cut4 = lambda v: v.reshape(NZ, NX, rows, v.shape[1])
    c1, c2, gu, pq = early(gate_pre, up_pre, upstream, factors)
    early_out = (cut4(c1), cut4(c2), cut4(pq))
    tot = (after(local, c1) + across) + (ahead_y + behind)
    weights = (gate_weight, up_weight, a_down, probe_a)
    blocks = [(k, 2) for k in range(NZ)] + [(4, j) for j in range(NX)]
    blocks += [("p", n, x) for n in range(2) for x in range(NX)]
    a2, b4 = ahead(
        blocks, ((0, 8, 0), (8, 4, ca)), place, early_out, tot, factors, *weights, ca, "send_first", rank_blocks=12
    )
    xs = send(go_x, *a2)
    zs = send(go_z, *b4)

    blocks = [(k, j) for j in (1, 3) for k in range(NZ)]
    a1, a3 = ahead(
        blocks, ((0, 8, 0), (8, 8, 0)), place, early_out, after(tot, *a2), factors, *weights, ca, "send_second"
    )
    blocks = [(k, j) for k in (3, 5) for j in range(NX)]
    b3, b5 = ahead(
        blocks, ((0, 4, ca), (4, 4, ca)), place, early_out, after(tot, *a1), factors, *weights, ca, "send_third"
    )
    zr, zl = together(after(zs[0], *b3), zs[1])
    zo = together(cat1(b3[0] + zr, b3[1]), cat1(b5[0], b5[1] + zl))
    zs = send(go_z, *zo)

    kept = a1[0].shape[0]
    xr, xl = together(after(xs[0], *zo), xs[1])
    own, beside, behind = together(a2[0][kept:], xl[kept:], xr[kept:])
    xo = together(
        cat0(cat1(a1[0] + xr[:kept], a1[1]), cat1(behind, behind)), cat1(a3[0], a3[1] + xl[:kept])
    )
    xs = send(go_x, *xo)

    *one, hg1, hu1 = body(
        (2, 6), place, c1, c2, gu, pq, up_pre, after(tot, *xo), factors, "body_first"
    )
    cb = gate_weight.shape[0] - ca
    b2, b6 = terms([one], (([(0, 0), (0, 1)], ca, cb, 2),), *weights, "terms_first")
    zp, zm = together(after(zs[0], b2), zs[1])
    zo = together(b2 + zp, b6 + zm)
    zs = send(go_z, *zo)

    *two, hg2, hu2 = body(
        (1, 7, 0, 3, 4, 5), place, c1, c2, gu, pq, up_pre, after(tot, *zo), factors, "body_second", LONG
    )
    at = [(1, 2), (1, 0), (0, 0), (1, 3), (1, 4), (1, 5), (0, 1), (1, 1)]
    a0, b1, b7, b0 = terms(
        [one, two],
        (([(source, (n, 0)) for source, n in at], 0, ca, 1), ([(1, 0), (1, 1), (1, 2)], ca, cb, 3)),
        *weights, "terms_second",
    )
    xp, xm = together(after(xs[0], a0), xs[1])
    asum = a0 + xp[:kept] + xm
    part = (own + xp[kept:, :own.shape[1]]) + (beside + behind)

    cut = lambda v, k: v[k * rows:(k + 1) * rows]
    t = {k: cut(asum, k) for k in range(NZ)}
    upper = rows // 2
    zp, zm = together(after(zs[0], asum), zs[1])
    zo = together(cat0(b1 + zp, t[4][:upper]), cat0(b7 + zm, t[4][upper:]))
    zs = send(go_z, *zo)
    hvp_b = cat0(hg1 + hg2, hu1 + hu2)
    hvp_b = hvp_b + swap_core(after(hvp_b, *zo))
    part_z = pair_z(after(part, hvp_b), 4)
    zp, zm = together(*zs)
    part = part + after(part_z, zp)

    kept = b0.shape[0]
    double = cat1(part, part)
    ao = together(
        cat0(t[3][:upper] + zp[kept:], t[3][upper:], t[1], double),
        cat0(t[5][:upper], t[5][upper:] + zm[kept:], t[7], double),
    )
    az = send(go_z, *ao)
    bsum = b0 + zp[:kept] + zm[:kept]
    quarter = {j: cut(bsum, j) for j in range(NX)}
    bo = together(quarter[1], quarter[3], part)
    bx = send(go_x, bo[0], bo[1])
    part_z = pair_z(bo[2], 2)

    ap, am = together(*az)
    ao = together(t[2] + ap[:rows], t[6] + am[:rows])
    az = go_z(ao[0], 2), go_z(ao[1], -2)
    far = go_x(after(quarter[2], *ao), 2)
    width = part.shape[1]
    part = (part + after(part_z, *ao, *bx)) + (ap[2 * rows:, :width] + am[2 * rows:, :width])
    p1, p2, p3 = go_y(part, -1), go_y(part, 2), go_y(part, 1)
    right = (quarter[0] + far) + (bx[0] + bx[1])
    left = (t[0] + ap[rows:2 * rows] + am[rows:2 * rows]) + (az[0] + az[1])
    input_tangent = cat1(left, right)

    hvp_a = width_sum(place, (after(part, *az), p1, p2, p3), inputs)
    hvp_a = hvp_a + swap_core(hvp_a)

    token_count = tokens * lax.axis_size("dp")
    scale_b = math.sqrt(token_count)
    scale_a = math.sqrt(token_count * FF)
    next_a = 2.0 * probe_a.astype(F32) - hvp_a / scale_a
    next_bg = 2.0 * probe_bg.astype(F32) - hvp_b[:16] / scale_b
    next_bu = 2.0 * probe_bu.astype(F32) - hvp_b[16:] / scale_b
    return (input_tangent, next_a, next_bg, next_bu)


def solution(mesh):
    return jax.shard_map(
        shards,
        mesh=mesh,
        in_specs=(
            P("dp", "inp"),
            P("dp", "out"),
            P("dp", "out"),
            P("dp", "out"),
            P("inp", "out"),
            P("inp", "out"),
            P(None, "inp"),
            P(None, "out"),
            P(None, "out"),
            P(None, "inp"),
            P(None, "out"),
            P(None, "out"),
        ),
        out_specs=(P(("dp", "out"), "inp"), P(None, "inp"), P(None, "out"), P(None, "out")),
        check_vma=False,
    )
```

```python
import functools
import math

import jax
import jax.numpy as jnp
from jax import lax
from jax.experimental import pallas as pl
from jax.experimental.pallas import tpu as pltpu
from jax.sharding import PartitionSpec as P

FF = 28672
NX, NZ = 4, 8
F32, BF16 = jnp.float32, jnp.bfloat16
LANES = 128


def dot_nt(left, right):
    return lax.dot_general(left, right, (((1,), (1,)), ((), ())), preferred_element_type=F32)


def dot_nn(left, right):
    return lax.dot_general(left, right, (((1,), (0,)), ((), ())), preferred_element_type=F32)


def dot_tn(left, right):
    return lax.dot_general(left, right, (((0,), (0,)), ((), ())), preferred_element_type=F32)


def split2(value):
    high = value.astype(BF16)
    return high, (value - high.astype(F32)).astype(BF16)


def split3(value):
    high = value.astype(BF16)
    rest = value - high.astype(F32)
    mid = rest.astype(BF16)
    return high, mid, (rest - mid.astype(F32)).astype(BF16)


def params(mib=26):
    return pltpu.CompilerParams(vmem_limit_bytes=mib * 1024 * 1024)


VMEM = pl.BlockSpec(memory_space=pltpu.VMEM)
SMEM = pl.BlockSpec(memory_space=pltpu.SMEM)
COST = pl.CostEstimate(flops=1000, bytes_accessed=1000, transcendentals=0)
LONG = pl.CostEstimate(flops=24_000_000_000, bytes_accessed=90_000_000, transcendentals=0)


def early_tables(rg, ru, bg_ref, bu_ref, pg_ref, pu_ref):
    for ref, first, second in ((rg, pg_ref, bg_ref), (ru, pu_ref, bu_ref)):
        ref[...] = jnp.zeros_like(ref)
        ref[0:16] = first[...]
        ref[16:32] = second[...]


def tangent_tables(bst, rp, bg_ref, bu_ref, pg_ref, pu_ref):
    width = bg_ref.shape[1]
    for n in range(0, 96, 32):
        bst[n:n + 16, :width] = bg_ref[...]
        bst[n:n + 16, width:] = bu_ref[...]
        bst[n + 16:n + 32, :width] = pg_ref[...]
        bst[n + 16:n + 32, width:] = pu_ref[...]
    rp[...] = jnp.zeros_like(rp)
    rp[0, 0:16] = bg_ref[...]
    rp[1, 0:16] = bu_ref[...]


def rank_table(aa, a_ref, pa_ref):
    aa[...] = jnp.zeros_like(aa)
    for n in (0, 32):
        aa[n:n + 16] = a_ref[...]
        aa[n + 16:n + 32] = pa_ref[...]


def elementwise(g, u, dy):
    g, u, dy = g.astype(F32), u.astype(F32), dy.astype(F32)
    sig = 1.0 / (1.0 + jnp.exp(-g))
    s = g * sig
    c1 = dy * (sig + (s - s * sig))
    gu = dy * s
    c2 = u * ((1.0 - sig) * (c1 + c1 - gu))
    return c1, c2, c1 * u, gu


def rank_terms(gg, gu, rg, ru):
    gg_hi, gg_lo = split2(gg)
    gu_hi, gu_lo = split2(gu)
    return (dot_nt(gg_hi, rg) + dot_nt(gg_lo, rg)) + (dot_nt(gu_hi, ru) + dot_nt(gu_lo, ru))


def tangent_math(both, c1, c2, pq, rpg, rpu):
    width = c1.shape[1]
    tang_g, tang_u = both[:, :width], both[:, width:]
    tgg = (tang_u * c1 + c2 * tang_g).astype(BF16)
    tgu = (c1 * tang_g).astype(BF16)
    pq = pq + (dot_nt(tgg, rpg) + dot_nt(tgu, rpu))
    high = pq.astype(BF16).astype(F32)
    return tgg, tgu, pq, (high + pltpu.roll(pq - high, 32, 1)).astype(BF16)


def body_kernel(place, c1_ref, c2_ref, gu_ref, pq_ref, u_ref, tot_ref, bg_ref, bu_ref, pg_ref, pu_ref,
                tgg_ref, tgu_ref, pqs_ref, hg_ref, hu_ref, bst, rp):
    first = pl.program_id(0) == 0

    @pl.when(first)
    def _():
        tangent_tables(bst, rp, bg_ref, bu_ref, pg_ref, pu_ref)

    c1 = c1_ref[...]
    tot = tot_ref[...]
    both = dot_tn(jnp.concatenate(split3(tot), axis=0), bst[...])
    tgg, tgu, _, full = tangent_math(both, c1, c2_ref[...], pq_ref[...], rp[0], rp[1])
    rows = tgg.shape[0] // NX
    for xx in range(NX):
        j = lax.rem(xx - place[1] + NX, NX)
        part = slice(xx * rows, (xx + 1) * rows)
        tgg_ref[0, j] = tgg[part]
        tgu_ref[0, j] = tgu[part]
        pqs_ref[0, j] = full[part]

    t_hi, t_lo = split2(tot)
    xv = jnp.concatenate([t_hi[:16], t_lo[:16]], axis=0)
    xa = jnp.concatenate([t_hi[16:], t_lo[16:]], axis=0)

    def both_terms(grad, tan):
        hi, lo = split2(grad)
        sums = dot_nn(xv, hi) + dot_nn(xa, tan)
        return sums[:16] + sums[16:] + dot_nn(xv[:16], lo)

    hg = both_terms(c1 * u_ref[...].astype(F32), tgg)
    hu = both_terms(gu_ref[...], tgu)

    @pl.when(first)
    def _():
        hg_ref[...] = hg
        hu_ref[...] = hu

    @pl.when(jnp.logical_not(first))
    def _():
        hg_ref[...] += hg
        hu_ref[...] += hu


def body(order, place, c1, c2, gu, pq, u, tot, factors, name, cost=COST):
    tokens, width = u.shape
    block = tokens // NZ
    rows = block // NX

    def nat(i, s):
        k = order[-1]
        for n, value in enumerate(order[:-1]):
            k = jnp.where(i == n, value, k)
        return lax.rem(k + s[0], NZ)

    row = pl.BlockSpec((block, width), lambda i, s: (nat(i, s), 0))
    rel = lambda n: pl.BlockSpec((1, NX, rows, n), lambda i, s: (i, 0, 0, 0))
    rank = pl.BlockSpec((16, width), lambda i, s: (0, 0))
    return pl.pallas_call(
        body_kernel,
        grid_spec=pltpu.PrefetchScalarGridSpec(
            num_scalar_prefetch=1,
            grid=(len(order),),
            in_specs=[
                row, row, row,
                pl.BlockSpec((block, LANES), lambda i, s: (nat(i, s), 0)),
                row,
                pl.BlockSpec((32, block), lambda i, s: (0, nat(i, s))),
                rank, rank, rank, rank,
            ],
            out_specs=[rel(width), rel(width), rel(LANES), rank, rank],
            scratch_shapes=[pltpu.VMEM((96, 2 * width), BF16), pltpu.VMEM((2, LANES, width), BF16)],
        ),
        out_shape=[
            jax.ShapeDtypeStruct((len(order), NX, rows, width), BF16),
            jax.ShapeDtypeStruct((len(order), NX, rows, width), BF16),
            jax.ShapeDtypeStruct((len(order), NX, rows, LANES), BF16),
            jax.ShapeDtypeStruct((16, width), F32),
            jax.ShapeDtypeStruct((16, width), F32),
        ],
        compiler_params=params(20),
        cost_estimate=cost,
        name=name,
    )(place, c1, c2, gu, pq, u, tot, *factors)


def terms_kernel(sources, jobs, gw_ref, uw_ref, a_ref, pa_ref, *rest):
    ins, outs, aa = rest[:3 * sources], rest[3 * sources:-1], rest[-1]
    rank_table(aa, a_ref, pa_ref)
    step = 256
    done = 0
    for blocks, low, columns, parts in jobs:
        def left(which):
            got = [ins[3 * source + which][index].reshape(-1, ins[3 * source + which].shape[-1])
                   for source, index in blocks]
            return got[0] if len(got) == 1 else jnp.concatenate(got, axis=0)

        lg, lu, lp = left(0), left(1), left(2)
        n = lg.shape[0] // parts
        for c in range(0, columns, step):
            cols = slice(low + c, low + c + step)
            value = (dot_nt(lg, gw_ref[cols]) + dot_nt(lu, uw_ref[cols])) + dot_nn(lp, aa[:, cols])
            for m in range(parts):
                outs[done + m][:, c:c + step] = value[m * n:(m + 1) * n]
        done += parts


def terms(bodies, jobs, gw, uw, a_down, probe_a, name):
    nx, rows = bodies[0][0].shape[1:3]
    shapes = []
    for blocks, _, columns, parts in jobs:
        count = sum(bodies[source][0][index].size for source, index in blocks) // bodies[0][0].shape[-1]
        shapes += [jax.ShapeDtypeStruct((count // parts, columns), F32)] * parts
    flat = [v for three in bodies for v in three]
    return pl.pallas_call(
        functools.partial(terms_kernel, len(bodies), jobs),
        in_specs=[VMEM] * (4 + len(flat)),
        out_specs=[VMEM] * len(shapes),
        out_shape=shapes,
        scratch_shapes=[pltpu.VMEM((LANES, gw.shape[0]), BF16)],
        compiler_params=params(18),
        cost_estimate=COST,
        name=name,
    )(gw, uw, a_down, probe_a, *flat)


def early_kernel(g_ref, u_ref, dy_ref, bg_ref, bu_ref, pg_ref, pu_ref, c1_ref, c2_ref, gu_ref, pq_ref, rg, ru):
    early_tables(rg, ru, bg_ref, bu_ref, pg_ref, pu_ref)
    block = g_ref.shape[0] // 8
    for n in range(8):
        rows = slice(n * block, (n + 1) * block)
        c1, c2, gg, gu = elementwise(g_ref[rows], u_ref[rows], dy_ref[rows])
        c1_ref[rows] = c1
        c2_ref[rows] = c2
        gu_ref[rows] = gu
        pq_ref[rows] = rank_terms(gg, gu, rg[...], ru[...])


def early(g, u, dy, factors):
    tokens, width = g.shape
    wide = jax.ShapeDtypeStruct((tokens, width), F32)
    return pl.pallas_call(
        early_kernel,
        in_specs=[VMEM] * 7,
        out_specs=[VMEM] * 4,
        out_shape=[wide, wide, wide, jax.ShapeDtypeStruct((tokens, LANES), F32)],
        scratch_shapes=[pltpu.VMEM((LANES, width), BF16), pltpu.VMEM((LANES, width), BF16)],
        compiler_params=params(22),
        cost_estimate=COST,
        name="early",
    )(g, u, dy, *factors)


def block_at(place, block):
    if len(block) == 3:
        return 2 * place[2] + block[1], block[2]
    return lax.rem(place[0] + block[0], NZ), lax.rem(place[1] + block[1], NX)


def ahead_kernel(blocks, groups, rank_blocks, place, c1_ref, c2_ref, pq_ref, tot_ref, bg_ref, bu_ref,
                 pg_ref, pu_ref, gw_ref, uw_ref, a_ref, pa_ref, *rest):
    outs, (tot_rows, bst, rp, aa) = rest[:-4], rest[-4:]
    rows = tot_rows.shape[1]
    tot_rows[...] = tot_ref[...].T.reshape(tot_rows.shape)
    tangent_tables(bst, rp, bg_ref, bu_ref, pg_ref, pu_ref)
    rank_table(aa, a_ref, pa_ref)
    at = [block_at(place, block) for block in blocks]
    gather = lambda ref: jnp.concatenate([ref[z, x] for z, x in at], axis=0)
    tot = jnp.concatenate([tot_rows[z * NX + x] for z, x in at], axis=0)
    both = dot_nn(jnp.concatenate(split3(tot), axis=1), bst[...])
    tgg, tgu, pq, full = tangent_math(both, gather(c1_ref), gather(c2_ref), gather(pq_ref), rp[0], rp[1])
    if rank_blocks is not None:
        low = rank_blocks * rows
        for n in range(0, pq.shape[0] - low, LANES):
            turned = pq[low + n:low + n + LANES].T
            for ref in outs[:2]:
                ref[-8:, n:n + LANES] = turned[0:8]
                ref[-8:, 256 + n:256 + n + LANES] = turned[8:16]
    step = 256
    lows = sorted({low for _, _, low in groups})
    for low in lows:
        mine = [(g, start, count) for g, (start, count, at_low) in enumerate(groups) if at_low == low]
        base, total = mine[0][1], sum(count for _, _, count in mine)
        part = slice(base * rows, (base + total) * rows)
        half = outs[2 * mine[0][0]].shape[1]
        for c in range(0, 2 * half, step):
            cols = slice(low + c, low + c + step)
            value = (
                dot_nt(tgg[part], gw_ref[cols]) + dot_nt(tgu[part], uw_ref[cols])
            ) + dot_nn(full[part], aa[:, cols])
            for g, start, count in mine:
                first = (start - base) * rows
                outs[2 * g + c // half][:count * rows, c % half:c % half + step] = value[first:first + count * rows]


def ahead(blocks, groups, place, early_out, tot, factors, gw, uw, a, pa, ca, name, rank_blocks=None):
    rows, width = early_out[0].shape[2:]
    model = gw.shape[0]
    shapes = []
    for g, (_, count, low) in enumerate(groups):
        columns = model - ca if low else ca
        more = 8 if g == 0 and rank_blocks is not None else 0
        shapes += [jax.ShapeDtypeStruct((count * rows + more, columns // 2), F32)] * 2
    outs = pl.pallas_call(
        functools.partial(ahead_kernel, blocks, groups, rank_blocks),
        in_specs=[SMEM] + [VMEM] * 12,
        out_specs=[VMEM] * len(shapes),
        out_shape=shapes,
        scratch_shapes=[
            pltpu.VMEM((NZ * NX, rows, 32), F32),
            pltpu.VMEM((96, 2 * width), BF16),
            pltpu.VMEM((2, LANES, width), BF16),
            pltpu.VMEM((LANES, model), BF16),
        ],
        compiler_params=params(20),
        cost_estimate=COST,
        name=name,
    )(place, *early_out, tot, *factors, gw, uw, a, pa)
    return [tuple(outs[2 * g:2 * g + 2]) for g in range(len(groups))]


def width_kernel(place, p0_ref, p1_ref, p2_ref, p3_ref, x_ref, out_ref):
    quarter = p0_ref.shape[1] // 2
    total = None
    for n, ref in enumerate((p0_ref, p1_ref, p2_ref, p3_ref)):
        start = pl.multiple_of(lax.rem(place[2] + n, 4) * quarter, quarter)
        p = jnp.concatenate([ref[:, :quarter], ref[:, quarter:]], axis=0)
        part = dot_nn(jnp.concatenate(split3(p), axis=0), x_ref[pl.ds(start, quarter), :])
        part = part[:16] + (part[16:32] + part[32:])
        total = part if total is None else total + part
    out_ref[...] = total


def width_sum(place, quarters, inputs):
    return pl.pallas_call(
        width_kernel,
        in_specs=[SMEM] + [VMEM] * 5,
        out_specs=VMEM,
        out_shape=jax.ShapeDtypeStruct((16, inputs.shape[1]), F32),
        compiler_params=params(12),
        cost_estimate=COST,
        name="width_sum",
    )(place, *quarters, inputs)


def place_kernel(place_ref, out_ref):
    for n in range(3):
        out_ref[n] = place_ref[n]


def hand_on(place):
    return pl.pallas_call(
        place_kernel,
        in_specs=[SMEM],
        out_specs=SMEM,
        out_shape=jax.ShapeDtypeStruct((3,), jnp.int32),
        compiler_params=params(2),
        cost_estimate=LONG,
        name="hand_on",
    )(place)


def out_perm(dz, dx):
    return [(z * NX + x, ((z + dz) % NZ) * NX + (x + dx) % NX) for z in range(NZ) for x in range(NX)]


def go_x(value, d):
    return lax.ppermute(value, "out", out_perm(0, d))


def go_z(value, d):
    return lax.ppermute(value, "out", out_perm(d, 0))


def go_y(value, d):
    return lax.ppermute(value, "inp", [(i, (i + d) % 4) for i in range(4)])


def pair_x(value, mask):
    return lax.ppermute(value, "out", [(z * NX + x, z * NX + (x ^ mask)) for z in range(NZ) for x in range(NX)])


def pair_z(value, mask):
    return lax.ppermute(value, "out", [(z * NX + x, (z ^ mask) * NX + x) for z in range(NZ) for x in range(NX)])


def swap_core(value):
    return lax.ppermute(value, "dp", [(0, 1), (1, 0)])


def send(go, ahead_value, back_value):
    return go(ahead_value, 1), go(back_value, -1)


def together(*values):
    return lax.optimization_barrier(values)


def after(value, *others):
    return lax.optimization_barrier((value,) + others)[0]


def shards(inputs, gate_pre, up_pre, upstream, gate_weight, up_weight,
           a_down, b_gate, b_up, probe_a, probe_bg, probe_bu):
    tokens = inputs.shape[0]
    ca = gate_weight.shape[0] // 2
    at = lax.axis_index("out")
    place = jnp.stack([at >> 2, at & 3, lax.axis_index("inp")]).astype(jnp.int32)
    place = hand_on(place)
    cat0 = lambda *a: jnp.concatenate(a, axis=0)
    cat1 = lambda *a: jnp.concatenate(a, axis=1)

    local = dot_nt(after(cat0(probe_a, a_down), place), inputs)
    across, ahead_y, behind = go_y(local, 2), go_y(local, 1), go_y(local, -1)

    factors = (b_gate, b_up, probe_bg, probe_bu)
    rows = tokens // (NZ * NX)
    cut4 = lambda v: v.reshape(NZ, NX, rows, v.shape[1])
    c1, c2, gu, pq = early(gate_pre, up_pre, upstream, factors)
    early_out = (cut4(c1), cut4(c2), cut4(pq))
    tot = (after(local, c1) + across) + (ahead_y + behind)
    weights = (gate_weight, up_weight, a_down, probe_a)
    blocks = [(k, 2) for k in range(NZ)] + [(4, j) for j in range(NX)]
    blocks += [("p", n, x) for n in range(2) for x in range(NX)]
    a2, b4 = ahead(
        blocks, ((0, 8, 0), (8, 4, ca)), place, early_out, tot, factors, *weights, ca, "send_first", rank_blocks=12
    )
    xs = send(go_x, *a2)
    zs = send(go_z, *b4)

    blocks = [(k, j) for j in (1, 3) for k in range(NZ)]
    a1, a3 = ahead(
        blocks, ((0, 8, 0), (8, 8, 0)), place, early_out, after(tot, *a2), factors, *weights, ca, "send_second"
    )
    blocks = [(k, j) for k in (3, 5) for j in range(NX)]
    b3, b5 = ahead(
        blocks, ((0, 4, ca), (4, 4, ca)), place, early_out, after(tot, *a1), factors, *weights, ca, "send_third"
    )
    zr, zl = together(after(zs[0], *b3), zs[1])
    zo = together(cat1(b3[0] + zr, b3[1]), cat1(b5[0], b5[1] + zl))
    zs = send(go_z, *zo)

    kept = a1[0].shape[0]
    xr, xl = together(after(xs[0], *zo), xs[1])
    own, beside, behind = together(a2[0][kept:], xl[kept:], xr[kept:])
    xo = together(
        cat0(cat1(a1[0] + xr[:kept], a1[1]), cat1(behind, behind)), cat1(a3[0], a3[1] + xl[:kept])
    )
    xs = send(go_x, *xo)

    *one, hg1, hu1 = body(
        (2, 6), place, c1, c2, gu, pq, up_pre, after(tot, *xo), factors, "body_first"
    )
    cb = gate_weight.shape[0] - ca
    b2, b6 = terms([one], (([(0, 0), (0, 1)], ca, cb, 2),), *weights, "terms_first")
    zp, zm = together(after(zs[0], b2), zs[1])
    zo = together(b2 + zp, b6 + zm)
    zs = send(go_z, *zo)

    *two, hg2, hu2 = body(
        (1, 7, 0, 3, 4, 5), place, c1, c2, gu, pq, up_pre, after(tot, *zo), factors, "body_second", LONG
    )
    at = [(1, 2), (1, 0), (0, 0), (1, 3), (1, 4), (1, 5), (0, 1), (1, 1)]
    a0, b1, b7, b0 = terms(
        [one, two],
        (([(source, (n, 0)) for source, n in at], 0, ca, 1), ([(1, 0), (1, 1), (1, 2)], ca, cb, 3)),
        *weights, "terms_second",
    )
    hvp_b = after(cat0(hg1 + hg2, hu1 + hu2), a0)
    hvp_b = hvp_b + swap_core(hvp_b)
    xp, xm = together(after(xs[0], hvp_b), xs[1])
    asum = a0 + xp[:kept] + xm
    part = (own + xp[kept:, :own.shape[1]]) + (beside + behind)

    cut = lambda v, k: v[k * rows:(k + 1) * rows]
    t = {k: cut(asum, k) for k in range(NZ)}
    upper = rows // 2
    zp, zm = together(after(zs[0], asum), zs[1])
    zo = together(cat0(b1 + zp, t[4][:upper]), cat0(b7 + zm, t[4][upper:]))
    zs = send(go_z, *zo)
    part_z = pair_z(after(part, *zo), 4)
    zp, zm = together(*zs)
    part = part + after(part_z, zp)

    kept = b0.shape[0]
    double = cat1(part, part)
    ao = together(
        cat0(t[3][:upper] + zp[kept:], t[3][upper:], t[1], double),
        cat0(t[5][:upper], t[5][upper:] + zm[kept:], t[7], double),
    )
    az = send(go_z, *ao)
    bsum = b0 + zp[:kept] + zm[:kept]
    quarter = {j: cut(bsum, j) for j in range(NX)}
    bo = together(quarter[1], quarter[3], part)
    bx = send(go_x, bo[0], bo[1])
    part_z = pair_z(bo[2], 2)

    ap, am = together(*az)
    ao = together(t[2] + ap[:rows], t[6] + am[:rows])
    az = go_z(ao[0], 2), go_z(ao[1], -2)
    far = go_x(after(quarter[2], *ao), 2)
    width = part.shape[1]
    part = (part + after(part_z, *ao, *bx)) + (ap[2 * rows:, :width] + am[2 * rows:, :width])
    p1, p2, p3 = go_y(part, -1), go_y(part, 2), go_y(part, 1)
    right = (quarter[0] + far) + (bx[0] + bx[1])
    left = (t[0] + ap[rows:2 * rows] + am[rows:2 * rows]) + (az[0] + az[1])
    input_tangent = cat1(left, right)

    hvp_a = width_sum(place, (after(part, *az), p1, p2, p3), inputs)
    hvp_a = hvp_a + swap_core(hvp_a)

    token_count = tokens * lax.axis_size("dp")
    scale_b = math.sqrt(token_count)
    scale_a = math.sqrt(token_count * FF)
    next_a = 2.0 * probe_a.astype(F32) - hvp_a / scale_a
    next_bg = 2.0 * probe_bg.astype(F32) - hvp_b[:16] / scale_b
    next_bu = 2.0 * probe_bu.astype(F32) - hvp_b[16:] / scale_b
    return (input_tangent, next_a, next_bg, next_bu)


def solution(mesh):
    return jax.shard_map(
        shards,
        mesh=mesh,
        in_specs=(
            P("dp", "inp"),
            P("dp", "out"),
            P("dp", "out"),
            P("dp", "out"),
            P("inp", "out"),
            P("inp", "out"),
            P(None, "inp"),
            P(None, "out"),
            P(None, "out"),
            P(None, "inp"),
            P(None, "out"),
            P(None, "out"),
        ),
        out_specs=(P(("dp", "out"), "inp"), P(None, "inp"), P(None, "out"), P(None, "out")),
        check_vma=False,
    )
```
